32 devices in a mesh: dp: 16 (over z, y, core), tensor: 2 (over x).
Axes of the slice: x: 2, y: 2, z: 4, core: 2. Of those that a mesh axis runs over, the one named last changes fastest.
Arguments:
- inputs: float32 [16384, 768], P('dp'), may hold values from -6 to 6
- pair_lengths: int32 [32, 3], P('dp'), may hold values from 0 to 464, as said below
- first_norm_gain: float32 [768], replicated, may hold values from 0.1 to 1.9
- first_norm_bias: float32 [768], replicated, may hold values from -1.75 to 1.75
- w_qkv: bfloat16 [768, 3, 768], P(None, None, 'tensor'), may hold values from -0.3125 to 0.3125
- b_qv: float32 [2, 768], P(None, 'tensor'), may hold values from -3 to 3
- w_out: bfloat16 [768, 768], P('tensor'), may hold values from -0.875 to 0.875
- b_out: float32 [768], replicated, may hold values from -3 to 3
- second_norm_gain: float32 [768], replicated, may hold values from 0.1 to 1.9
- second_norm_bias: float32 [768], replicated, may hold values from -1.75 to 1.75
- w_up: bfloat16 [768, 3072], P(None, 'tensor'), may hold values from -0.21875 to 0.21875
- b_up: float32 [3072], P('tensor'), may hold values from -3 to 3
- w_down: bfloat16 [3072, 768], P('tensor'), may hold values from -0.109375 to 0.109375
- b_down: float32 [768], replicated, may hold values from -3 to 3
- cotangent: float32 [16384, 768], P('dp'), may hold values from -6 to 6
Outputs:
- output: float32 [16384, 768], P('dp')
- gradient_of_input: float32 [16384, 768], P('dp')
- first_norm_gain_gradient: float32 [768], replicated
- grad_ln1_bias: float32 [768], replicated
- grad_w_qkv: float32 [768, 3, 768], P(None, None, 'tensor')
- grad_b_qv: float32 [2, 768], P(None, 'tensor')
- grad_w_out: float32 [768, 768], P('tensor')
- grad_b_out: float32 [768], replicated
- second_norm_gain_gradient: float32 [768], replicated
- grad_ln2_bias: float32 [768], replicated
- grad_w_up: float32 [768, 3072], P(None, 'tensor')
- grad_b_up: float32 [3072], P('tensor')
- grad_w_down: float32 [3072, 768], P('tensor')
- grad_b_down: float32 [768], replicated
The draws below stay inside these ranges and needn't reach their ends.
Inputs may be any that keep to these rules, and one draw needn't show every extreme that they name: `pair_lengths`: each row lists the rows of the image-text pairs packed into one sequence in order: two or three pairs of 48 rows or more, a 0 in the last column where there is no third pair; a row sums to at most 512, the rest of the sequence is padding.
All inputs are finite; a program needn't handle non-finite values.
Results may differ from the reference program's by a relative error of at most 0.012.
The reference program's roundings to bfloat16 on the way count: a program that leaves them out, or rounds other values in their place, can miss the bound.
Values sent between devices are 32-bit elements; how exact they have to be, the bound alone decides.
No kernel may reach another device: no remote copies, remote signals or barrier semaphores. Data moves between devices by JAX's collectives and lax.ppermute only.
A program may use at most 192 MiB of HBM per device.

```python
import math
import jax
import jax.numpy as jnp
from jax import lax

D = 768
HEADS = 12
HEAD_DIM = 64
FF = 3072
SEQ_LEN = 512
PAIR_MIN = 48
SEQS = 32
TOKENS = 16384


def draw_pair_lengths(key, part):
    key = jax.random.fold_in(key, 7)
    keys_all = jax.random.split(key, 4)
    pair_count = jax.random.randint(keys_all[0], (SEQS, 1), 2, 4)
    padding = jax.random.randint(keys_all[1], (SEQS, 1), 0, SEQ_LEN // 16 + 1)
    shares = jax.random.randint(keys_all[2], (SEQS, 3), 1, 9)
    slot_ids = lax.broadcasted_iota(jnp.int32, (SEQS, 3), 1)
    live_slot = slot_ids < pair_count
    shares = jnp.where(live_slot, shares, 0)
    spare_len = SEQ_LEN - padding - pair_count * PAIR_MIN
    extra_len = spare_len * shares // jnp.sum(shares, axis=1, keepdims=True)
    leftover = spare_len - jnp.sum(extra_len, axis=1, keepdims=True)
    extra_len = extra_len + jnp.where(slot_ids == 0, leftover, 0)
    lengths = jnp.where(live_slot, PAIR_MIN + extra_len, 0)
    chosen = jax.random.randint(keys_all[3], (), 0, SEQS)
    forced = jnp.where(slot_ids == 0, SEQ_LEN - PAIR_MIN, jnp.where(slot_ids == 1, PAIR_MIN, 0))
    row_ids = lax.broadcasted_iota(jnp.int32, (SEQS, 3), 0)
    return jnp.where(row_ids == chosen, forced, lengths).astype(jnp.int32)


def shard_levels(key, dims, shards, smallest, high):
    def one(position, parts):
        steps = jax.random.uniform(jax.random.fold_in(jax.random.fold_in(key, 6), position), (parts,), jnp.float32, smallest / len(shards), high / len(shards))
        return jnp.repeat(jnp.exp(steps), dims[position] // parts).reshape((-1,) + (1,) * (len(dims) - position - 1))

    gain = one(*shards[0])
    for cut in shards[1:]:
        gain = gain * one(*cut)
    return gain


def noise(key, extent, spread, limit, cuts=(), held_as=jnp.bfloat16):
    values = jax.random.normal(key, extent, jnp.float32) * spread
    if len(cuts) > 0:
        values = shard_levels(key, extent, cuts, -0.22, 0.18) * values
    return jnp.clip(values, min=-limit, max=limit).astype(held_as)


def setup_inputs(seed: int = 0) -> dict:
    key_list = jax.random.split(jax.random.key(seed), 16)
    return {
        "inputs": noise(key_list[0], (TOKENS, D), 1.0, 6.0, ((0, 16),), jnp.float32),
        "pair_lengths": draw_pair_lengths(jax.random.fold_in(key_list[15], 71), 0),
        "first_norm_gain": jnp.clip(1.0 + 0.18 * jax.random.normal(key_list[2], (D,), jnp.float32), 0.1, 1.9),
        "first_norm_bias": noise(key_list[3], (D,), 0.3, 1.75, (), jnp.float32),
        "w_qkv": noise(key_list[4], (D, 3, HEADS * HEAD_DIM), (D // 2) ** -0.5, 0.3125, ((2, 2),)),
        "b_qv": noise(key_list[5], (2, HEADS * HEAD_DIM), 0.5, 3.0, ((1, 2),), jnp.float32),
        "w_out": noise(key_list[6], (HEADS * HEAD_DIM, D), (HEADS * HEAD_DIM // 16) ** -0.5, 0.875, ((0, 2),)),
        "b_out": noise(key_list[7], (D,), 0.5, 3.0, (), jnp.float32),
        "second_norm_gain": jnp.clip(1.0 + 0.18 * jax.random.normal(key_list[8], (D,), jnp.float32), 0.1, 1.9),
        "second_norm_bias": noise(key_list[9], (D,), 0.3, 1.75, (), jnp.float32),
        "w_up": noise(key_list[10], (D, FF), D ** -0.5, 0.21875, ((1, 2),)),
        "b_up": noise(key_list[11], (FF,), 0.5, 3.0, ((0, 2),), jnp.float32),
        "w_down": noise(key_list[12], (FF, D), FF ** -0.5, 0.109375, ((0, 2),)),
        "b_down": noise(key_list[13], (D,), 0.5, 3.0, (), jnp.float32),
        "cotangent": noise(key_list[14], (TOKENS, D), 1.0, 6.0, ((0, 16),), jnp.float32),
    }


EPS = 1e-06

@jax.custom_vjp
def low(v):
    return lax.optimization_barrier(v.astype(jnp.bfloat16)).astype(jnp.float32)

@jax.custom_vjp
def low_back(v):
    return v

def low_keep(v):
    return (low(v), None)

def low_pass(kept, grad):
    return (grad,)

def back_keep(v):
    return (v, None)

def back_low(kept, grad):
    return (low(grad),)
low.defvjp(low_keep, low_pass)
low_back.defvjp(back_keep, back_low)

def layer_norm(values, norm_gain_factor, shift):
    row_mean = lax.optimization_barrier(jnp.mean(values, -1, keepdims=True))
    centred = values - row_mean
    inverse_deviation = lax.rsqrt(lax.optimization_barrier(jnp.mean(centred * centred, -1, keepdims=True)) + EPS)
    return centred * inverse_deviation * norm_gain_factor + shift

def exact_dot(left, right):
    return jnp.dot(left, right, precision=lax.Precision.HIGHEST)

def segment_ids(pair_lengths, seq_len):
    pair_ends = jnp.cumsum(pair_lengths, axis=1)
    places = lax.broadcasted_iota(jnp.int32, (1, seq_len, 1), 1)
    return lax.optimization_barrier(jnp.sum((places >= pair_ends[:, None, :]).astype(jnp.int32), axis=2))

def attend(blocks):
    query_block, key_block, value_block, seg_block = blocks
    scale_factor = 1.0 / math.sqrt(HEAD_DIM)
    raw_scores = jnp.einsum('gqhd,gkhd->ghqk', query_block, key_block, precision=lax.Precision.HIGHEST)
    scores = low_back(raw_scores * scale_factor)
    same_seg = seg_block[:, None, :, None] == seg_block[:, None, None, :]
    probs = jax.nn.softmax(jnp.where(same_seg, scores, -1e+30), axis=-1)
    return jnp.einsum('ghqk,gkhd->gqhd', low(probs), value_block, precision=lax.Precision.HIGHEST)

def forward(inputs, first_norm_gain, first_norm_bias, w_qkv, b_qv, w_out, b_out, second_norm_gain, second_norm_bias, w_up, b_up, w_down, b_down, seg_groups):
    att_width = HEADS * HEAD_DIM
    token_count = inputs.shape[0]
    normalized_rows = low(layer_norm(inputs, first_norm_gain, first_norm_bias))
    projected = exact_dot(normalized_rows, w_qkv.reshape(D, 3 * att_width)).reshape(token_count, 3, att_width)
    bias_rows = jnp.stack([b_qv[0], jnp.zeros_like(b_qv[0]), b_qv[1]])
    qkv_rows = low_back(low(projected + bias_rows))
    groups = seg_groups.shape[0]
    per_group = seg_groups.shape[1]
    split_heads = qkv_rows.reshape(groups, per_group, SEQ_LEN, 3, HEADS, HEAD_DIM)
    attended = lax.map(jax.checkpoint(attend), (split_heads[:, :, :, 0], split_heads[:, :, :, 1], split_heads[:, :, :, 2], seg_groups))
    attended = low_back(low(attended.reshape(token_count, att_width)))
    residual_middle = inputs + low_back(exact_dot(attended, w_out)) + b_out
    second_normalized_rows = low(layer_norm(residual_middle, second_norm_gain, second_norm_bias))
    pre_act = low_back(exact_dot(second_normalized_rows, w_up) + b_up)
    hidden = low(jax.nn.gelu(pre_act, approximate=False))
    return residual_middle + low_back(exact_dot(hidden, w_down)) + b_down

def reference(inputs, pair_lengths, first_norm_gain, first_norm_bias, w_qkv, b_qv, w_out, b_out, second_norm_gain, second_norm_bias, w_up, b_up, w_down, b_down, cotangent):
    per_group = math.gcd(SEQS, max(1, 4096 // SEQ_LEN))
    seg_groups = segment_ids(pair_lengths, SEQ_LEN).reshape(SEQS // per_group, per_group, SEQ_LEN)
    floats = (inputs, first_norm_gain, first_norm_bias, w_qkv.astype(jnp.float32), b_qv, w_out.astype(jnp.float32), b_out, second_norm_gain, second_norm_bias, w_up.astype(jnp.float32), b_up, w_down.astype(jnp.float32), b_down)

    def layer_fn(*params):
        return forward(*params, seg_groups)
    output, pullback = jax.vjp(layer_fn, *floats)
    grads = pullback(cotangent)
    return (output, grads[0], grads[1], grads[2], grads[3], grads[4], grads[5], grads[6], grads[7], grads[8], grads[9], grads[10], grads[11], grads[12])
```

```python
import math

import jax
import jax.numpy as jnp
from jax import lax
from jax.sharding import PartitionSpec as P

HEAD_DIM = 64


EPS = 1e-06


def apply_layer_norm(values):
    row_mean = jnp.mean(values, -1, keepdims=True)
    centred = values - row_mean
    inverse_deviation = lax.rsqrt(jnp.mean(centred * centred, -1, keepdims=True) + EPS)
    return (centred * inverse_deviation, inverse_deviation)


def norm_backward_pass(
    normalized_gradient, norm_gain_factor, standardized_input, inverse_deviation
):
    scaled_rows = normalized_gradient * norm_gain_factor
    return inverse_deviation * (
        scaled_rows
        - jnp.mean(scaled_rows, -1, keepdims=True)
        - standardized_input * jnp.mean(scaled_rows * standardized_input, -1, keepdims=True)
    )


def segment_ids(pair_lengths, seq_len):
    first_end = pair_lengths[:, 0]
    second_end = first_end + pair_lengths[:, 1]
    pair_ends = jnp.stack([first_end, second_end, second_end + pair_lengths[:, 2]], axis=1)
    places = lax.broadcasted_iota(jnp.int32, (1, seq_len, 1), 1)
    return jnp.sum((places >= pair_ends[:, None, :]).astype(jnp.int32), axis=2)


def gelu_exact(values):
    return jax.nn.gelu(values, approximate=False)


def masked_scores(query_block, key_block, seg_block, scale_factor):
    raw_scores = (
        jnp.einsum("gqhd,gkhd->ghqk", query_block, key_block, preferred_element_type=jnp.float32)
        * scale_factor
    )
    same_seg = seg_block[:, None, :, None] == seg_block[:, None, None, :]
    return jnp.where(same_seg, raw_scores, -1e30)


def attend_forward(blocks, scale_factor):
    query_block, key_block, value_block, seg_block = blocks
    scores = masked_scores(query_block, key_block, seg_block, scale_factor)
    row_max = jnp.max(scores, -1, keepdims=True)
    exps = jnp.exp(scores - row_max)
    exp_total = jnp.sum(exps, -1, keepdims=True)
    weights = (exps / exp_total).astype(jnp.bfloat16)
    mixed = jnp.einsum("ghqk,gkhd->gqhd", weights, value_block, preferred_element_type=jnp.float32)
    return (mixed.astype(jnp.bfloat16), row_max + jnp.log(exp_total))


def attend_backward(blocks, scale_factor):
    query_block, key_block, value_block, seg_block, log_total, grad_mixed = blocks
    scores = masked_scores(query_block, key_block, seg_block, scale_factor)
    probs = jnp.exp(scores - log_total)
    probs_bf = probs.astype(jnp.bfloat16)
    grad_value = jnp.einsum(
        "ghqk,gqhd->gkhd", probs_bf, grad_mixed, preferred_element_type=jnp.float32
    )
    grad_probs = jnp.einsum(
        "gqhd,gkhd->ghqk", grad_mixed, value_block, preferred_element_type=jnp.float32
    )
    row_dot = jnp.sum(grad_probs * probs, -1, keepdims=True)
    grad_scores = (probs * (grad_probs - row_dot)).astype(jnp.bfloat16)
    grad_query = (
        jnp.einsum("ghqk,gkhd->gqhd", grad_scores, key_block, preferred_element_type=jnp.float32)
        * scale_factor
    )
    grad_key = (
        jnp.einsum("ghqk,gqhd->gkhd", grad_scores, query_block, preferred_element_type=jnp.float32)
        * scale_factor
    )
    return (grad_query, grad_key, grad_value)


def pack(arrays):
    return jnp.concatenate([piece.reshape(-1) for piece in arrays])


def unpack(flat, arrays):
    pieces = []
    offset = 0
    for piece in arrays:
        pieces.append(flat[offset : offset + piece.size].reshape(piece.shape))
        offset += piece.size
    return tuple(pieces)


def shards(
    inputs,
    pair_lengths,
    first_norm_gain,
    first_norm_bias,
    w_qkv,
    b_qv,
    w_out,
    b_out,
    second_norm_gain,
    second_norm_bias,
    w_up,
    b_up,
    w_down,
    b_down,
    cotangent,
):
    attn_shapes = (w_qkv, w_out, b_qv, b_out, first_norm_gain, first_norm_bias)
    mlp_shapes = (w_up, w_down, b_up, b_down, second_norm_gain, second_norm_bias)
    seq_count = pair_lengths.shape[0]
    token_count, width = inputs.shape
    seq_len = token_count // seq_count
    att_width = w_qkv.shape[2]
    head_count = att_width // HEAD_DIM
    scale_factor = 1.0 / math.sqrt(HEAD_DIM)
    per_group = math.gcd(seq_count, max(1, 512 // seq_len))
    group_count = seq_count // per_group
    seg_groups = segment_ids(pair_lengths, seq_len).reshape(group_count, per_group, seq_len)
    first_standardized, first_inverse_deviation = apply_layer_norm(inputs)
    normalized_rows = (first_standardized * first_norm_gain + first_norm_bias).astype(jnp.bfloat16)
    projected = jnp.dot(
        normalized_rows, w_qkv.reshape(width, 3 * att_width), preferred_element_type=jnp.float32
    )
    bias_rows = jnp.stack([b_qv[0], jnp.zeros_like(b_qv[0]), b_qv[1]])
    qkv_rows = (projected.reshape(token_count, 3, att_width) + bias_rows).astype(jnp.bfloat16)
    split_heads = qkv_rows.reshape(group_count, per_group, seq_len, 3, head_count, HEAD_DIM)
    query_all = split_heads[:, :, :, 0]
    key_all = split_heads[:, :, :, 1]
    value_all = split_heads[:, :, :, 2]

    def forward_block(blocks):
        return attend_forward(blocks, scale_factor)

    attended, log_totals = lax.map(forward_block, (query_all, key_all, value_all, seg_groups))
    attended = attended.reshape(token_count, att_width)
    branch = jnp.dot(attended, w_out, preferred_element_type=jnp.float32)
    branch_total = lax.all_gather(
        lax.psum_scatter(branch, "tensor", scatter_dimension=0, tiled=True),
        "tensor",
        axis=0,
        tiled=True,
    )
    residual_middle = inputs + branch_total + b_out
    second_standardized, second_inverse_deviation = apply_layer_norm(residual_middle)
    second_normalized_rows = (second_standardized * second_norm_gain + second_norm_bias).astype(
        jnp.bfloat16
    )
    pre_act = jnp.dot(second_normalized_rows, w_up, preferred_element_type=jnp.float32) + b_up
    activated, gelu_pull = jax.vjp(gelu_exact, pre_act)
    hidden_bf = activated.astype(jnp.bfloat16)
    down_part = jnp.dot(hidden_bf, w_down, preferred_element_type=jnp.float32)
    down_total = lax.all_gather(
        lax.psum_scatter(down_part, "tensor", scatter_dimension=0, tiled=True),
        "tensor",
        axis=0,
        tiled=True,
    )
    output = residual_middle + down_total + b_down
    out_bf = cotangent.astype(jnp.bfloat16)
    grad_b_down = jnp.sum(cotangent, 0)
    grad_w_down = jnp.einsum("tf,td->fd", hidden_bf, out_bf, preferred_element_type=jnp.float32)
    grad_hidden = jnp.einsum("td,fd->tf", out_bf, w_down, preferred_element_type=jnp.float32)
    grad_pre = gelu_pull(grad_hidden)[0].astype(jnp.bfloat16)
    grad_b_up = jnp.sum(grad_pre, 0, dtype=jnp.float32)
    grad_w_up = jnp.einsum(
        "td,tf->df", second_normalized_rows, grad_pre, preferred_element_type=jnp.float32
    )
    entry_two = jnp.einsum("tf,df->td", grad_pre, w_up, preferred_element_type=jnp.float32)
    second_normalized_gradient = lax.all_gather(
        lax.psum_scatter(entry_two, "tensor", scatter_dimension=0, tiled=True),
        "tensor",
        axis=0,
        tiled=True,
    )
    second_norm_gain_gradient = jnp.sum(second_normalized_gradient * second_standardized, 0)
    grad_ln2_bias = jnp.sum(second_normalized_gradient, 0)
    middle_state_gradient = cotangent + norm_backward_pass(
        second_normalized_gradient, second_norm_gain, second_standardized, second_inverse_deviation
    )
    mlp_flat = pack(
        (grad_w_up, grad_w_down, grad_b_up, grad_b_down, second_norm_gain_gradient, grad_ln2_bias)
    )
    mlp_part = lax.psum_scatter(mlp_flat, "dp", scatter_dimension=0, tiled=True)
    mlp_total = lax.all_gather(mlp_part, "dp", axis=0, tiled=True)
    grad_b_out = jnp.sum(middle_state_gradient, 0)
    middle_bf = middle_state_gradient.astype(jnp.bfloat16)
    grad_w_out = jnp.einsum("ta,td->ad", attended, middle_bf, preferred_element_type=jnp.float32)
    grad_attended = jnp.einsum(
        "td,ad->ta", middle_bf, w_out, preferred_element_type=jnp.float32
    ).astype(jnp.bfloat16)
    grad_heads = grad_attended.reshape(group_count, per_group, seq_len, head_count, HEAD_DIM)

    def backward_block(blocks):
        return attend_backward(blocks, scale_factor)

    grad_query, grad_key, grad_value = lax.map(
        backward_block, (query_all, key_all, value_all, seg_groups, log_totals, grad_heads)
    )
    grad_qkv = (
        jnp.stack([grad_query, grad_key, grad_value], axis=3)
        .reshape(token_count, 3, att_width)
        .astype(jnp.bfloat16)
    )
    grad_b_qv = jnp.stack(
        [
            jnp.sum(grad_qkv[:, 0], 0, dtype=jnp.float32),
            jnp.sum(grad_qkv[:, 2], 0, dtype=jnp.float32),
        ]
    )
    grad_w_qkv = jnp.einsum(
        "td,tca->dca", normalized_rows, grad_qkv, preferred_element_type=jnp.float32
    )
    entry_one = jnp.einsum("tca,dca->td", grad_qkv, w_qkv, preferred_element_type=jnp.float32)
    normalized_gradient = lax.all_gather(
        lax.psum_scatter(entry_one, "tensor", scatter_dimension=0, tiled=True),
        "tensor",
        axis=0,
        tiled=True,
    )
    first_norm_gain_gradient = jnp.sum(normalized_gradient * first_standardized, 0)
    grad_ln1_bias = jnp.sum(normalized_gradient, 0)
    gradient_of_input = middle_state_gradient + norm_backward_pass(
        normalized_gradient, first_norm_gain, first_standardized, first_inverse_deviation
    )
    attn_flat = pack(
        (grad_w_qkv, grad_w_out, grad_b_qv, grad_b_out, first_norm_gain_gradient, grad_ln1_bias)
    )
    attn_part = lax.psum_scatter(attn_flat, "dp", scatter_dimension=0, tiled=True)
    attn_summed = unpack(lax.all_gather(attn_part, "dp", axis=0, tiled=True), attn_shapes)
    mlp_summed = unpack(mlp_total, mlp_shapes)
    return (
        output,
        gradient_of_input,
        attn_summed[4],
        attn_summed[5],
        attn_summed[0],
        attn_summed[2],
        attn_summed[1],
        attn_summed[3],
        mlp_summed[4],
        mlp_summed[5],
        mlp_summed[0],
        mlp_summed[2],
        mlp_summed[1],
        mlp_summed[3],
    )


def solution(mesh):
    placed = (
        P("dp", None),
        P("dp", None),
        P(),
        P(),
        P(None, None, "tensor"),
        P(None, "tensor"),
        P("tensor", None),
        P(),
        P(),
        P(),
        P(None, "tensor"),
        P("tensor"),
        P("tensor", None),
        P(),
        P("dp", None),
    )
    return jax.shard_map(
        shards,
        mesh=mesh,
        in_specs=placed,
        out_specs=(
            P("dp", None),
            P("dp", None),
            P(),
            P(),
            P(None, None, "tensor"),
            P(None, "tensor"),
            P("tensor", None),
            P(),
            P(),
            P(),
            P(None, "tensor"),
            P("tensor"),
            P("tensor", None),
            P(),
        ),
        check_vma=False,
    )
```

```python
import functools
import math

import jax
import jax.numpy as jnp
from jax import lax
from jax.experimental import pallas as pl
from jax.experimental.pallas import tpu as pltpu
from jax.sharding import PartitionSpec as P

HEAD_DIM = 64
LANES = 128
EPS = 1e-06
MASKED = -1e30
VMEM_BYTES = 56 * 1024 * 1024
F32 = jnp.float32
BF16 = jnp.bfloat16
ERFC_P = 0.3925
ERFC_C = (
    0.2342248384381894,
    0.1104885068031651,
    0.6008554065531575,
    -0.5658356357906557,
    0.8411781949001069,
    -0.22091131771921121,
)


def dot(left, right):
    return lax.dot_general(left, right, (((1,), (0,)), ((), ())), preferred_element_type=F32)


def dot_bt(left, right):
    return lax.dot_general(left, right, (((1,), (1,)), ((), ())), preferred_element_type=F32)


def dot_at(left, right):
    return lax.dot_general(left, right, (((0,), (0,)), ((), ())), preferred_element_type=F32)


def standardize(values):
    row_mean = jnp.mean(values, -1, keepdims=True)
    centred = values - row_mean
    inverse_deviation = lax.rsqrt(jnp.mean(centred * centred, -1, keepdims=True) + EPS)
    return centred * inverse_deviation, inverse_deviation


def norm_pull(grad_normed, gain, xhat, inverse_deviation):
    scaled = grad_normed * gain
    return inverse_deviation * (
        scaled
        - jnp.mean(scaled, -1, keepdims=True)
        - xhat * jnp.mean(scaled * xhat, -1, keepdims=True)
    )


def segment_bias(lengths_ref, seq, seq_len):
    end_one = lengths_ref[seq, 0]
    end_two = end_one + lengths_ref[seq, 1]
    end_three = end_two + lengths_ref[seq, 2]

    def ids(shape, dim):
        place = lax.broadcasted_iota(jnp.int32, shape, dim)
        return (
            (place >= end_one).astype(jnp.int32)
            + (place >= end_two).astype(jnp.int32)
            + (place >= end_three).astype(jnp.int32)
        )

    same = ids((seq_len, seq_len), 0) == ids((seq_len, seq_len), 1)
    return jnp.where(same, 0.0, MASKED).astype(F32)


def head_only(block, half):
    lane = lax.broadcasted_iota(jnp.int32, block.shape, 1)
    mine = (lane < HEAD_DIM) if half == 0 else (lane >= HEAD_DIM)
    return jnp.where(mine, block, jnp.zeros_like(block))


def attention_forward_kernel(
    seq_ref, lengths_ref, rows_ref, w_ref, b_ref, gain_ref, shift_ref,
    normed_ref, qkv_ref, attended_ref, lse_ref, bias_ref,
):
    seq_len = rows_ref.shape[0]
    width = w_ref.shape[2]
    xhat, _ = standardize(rows_ref[...])
    normed = (xhat * gain_ref[...] + shift_ref[...]).astype(BF16)
    normed_ref[...] = normed
    scale = 1.0 / math.sqrt(HEAD_DIM)
    qkv_ref[0] = ((dot(normed, w_ref[0]) + b_ref[0:1]).astype(BF16).astype(F32) * scale).astype(BF16)
    qkv_ref[1] = dot(normed, w_ref[1]).astype(BF16)
    qkv_ref[2] = (dot(normed, w_ref[2]) + b_ref[1:2]).astype(BF16)
    bias_ref[...] = segment_bias(lengths_ref, seq_ref[0], seq_len)
    lane = lax.broadcasted_iota(jnp.int32, (seq_len, LANES), 1)
    stats = jnp.zeros((seq_len, LANES), F32)
    for pair in range(width // LANES):
        cols = slice(pair * LANES, (pair + 1) * LANES)
        query, key, value = qkv_ref[0, :, cols], qkv_ref[1, :, cols], qkv_ref[2, :, cols]
        mixed = None
        for half in range(2):
            scores = dot_bt(query, head_only(key, half)) + bias_ref[...]
            row_max = jnp.max(scores, -1, keepdims=True)
            exps = jnp.exp(scores - row_max)
            total = jnp.sum(exps, -1, keepdims=True)
            probs = (exps * (1.0 / total)).astype(BF16)
            part = dot(probs, head_only(value, half))
            mixed = part if mixed is None else mixed + part
            stats = jnp.where(lane == 2 * pair + half, row_max + jnp.log(total), stats)
        attended_ref[:, cols] = mixed.astype(BF16).astype(F32)
    lse_ref[...] = stats.T[: lse_ref.shape[0]]


def attention_forward(seq, lengths, rows, w_heads, b_qv, gain, shift, seq_len):
    width = rows.shape[1]
    heads_width = w_heads.shape[2]
    stat_rows = 8 * pl.cdiv(heads_width // HEAD_DIM, 8)
    whole = lambda *shape: pl.BlockSpec(shape, lambda i, s, n: (0,) * len(shape))
    return pl.pallas_call(
        attention_forward_kernel,
        out_shape=(
            jax.ShapeDtypeStruct((seq_len, width), BF16),
            jax.ShapeDtypeStruct((3, seq_len, heads_width), BF16),
            jax.ShapeDtypeStruct((seq_len, heads_width), F32),
            jax.ShapeDtypeStruct((stat_rows, seq_len), F32),
        ),
        grid_spec=pltpu.PrefetchScalarGridSpec(
            num_scalar_prefetch=2,
            grid=(1,),
            in_specs=[
                pl.BlockSpec((seq_len, width), lambda i, s, n: (s[0], 0)),
                whole(3, width, heads_width),
                whole(2, heads_width),
                whole(1, width),
                whole(1, width),
            ],
            out_specs=[
                whole(seq_len, width),
                whole(3, seq_len, heads_width),
                whole(seq_len, heads_width),
                whole(stat_rows, seq_len),
            ],
            scratch_shapes=[pltpu.VMEM((seq_len, seq_len), F32)],
        ),
        compiler_params=pltpu.CompilerParams(vmem_limit_bytes=VMEM_BYTES),
        cost_estimate=pl.CostEstimate(
            flops=2 * seq_len * heads_width * (3 * width + 8 * seq_len),
            bytes_accessed=4 * seq_len * width + 6 * width * heads_width,
            transcendentals=seq_len * seq_len * heads_width // HEAD_DIM,
        ),
        name="attention_forward",
    )(seq, lengths, rows, w_heads, b_qv, gain, shift)


def feed_forward_kernel(
    seq_ref, rows_ref, cot_ref, att_mine_ref, att_peer_ref, wo_mine_ref, wo_peer_ref, b_out_ref,
    gain_ref, shift_ref, w_up_ref, b_up_ref, w_down_ref,
    middle_ref, normed_ref, hidden_ref, grad_pre_ref, down_ref, grad_normed_ref, grad_b_up_ref,
):
    middle = (
        rows_ref[...]
        + dot(att_mine_ref[...].astype(BF16), wo_mine_ref[...])
        + dot(att_peer_ref[...].astype(BF16), wo_peer_ref[...].astype(BF16))
        + b_out_ref[...]
    )
    middle_ref[...] = middle
    xhat, _ = standardize(middle)
    normed = (xhat * gain_ref[...] + shift_ref[...]).astype(BF16)
    normed_ref[...] = normed
    cot = cot_ref[...].astype(BF16)

    @pl.when(pl.program_id(0) == 0)
    def _():
        grad_b_up_ref[...] = jnp.zeros_like(grad_b_up_ref)

    pre = dot(normed, w_up_ref[...]) + b_up_ref[...]
    size = jnp.abs(pre) * math.sqrt(0.5)
    t = 1.0 / (1.0 + ERFC_P * size)
    gauss = jnp.exp(-0.5 * (pre * pre))
    poly = ERFC_C[-1]
    for c in ERFC_C[-2::-1]:
        poly = poly * t + c
    tail = 0.5 * (poly * t) * gauss
    cdf = jnp.where(pre >= 0, 1.0 - tail, tail)
    hidden = (pre * cdf).astype(BF16)
    slope = cdf + pre * gauss * (1.0 / math.sqrt(2.0 * math.pi))
    hidden_ref[...] = hidden
    down_ref[...] = dot(hidden, w_down_ref[...])
    grad_pre = (dot_bt(cot, w_down_ref[...]) * slope).astype(BF16)
    grad_pre_ref[...] = grad_pre
    grad_b_up_ref[...] += jnp.sum(grad_pre.astype(F32), 0, keepdims=True)
    grad_normed_ref[...] = dot_bt(grad_pre, w_up_ref[...])


def feed_forward(seq, rows, cot, att_mine, att_peer, wo_mine, wo_peer, b_out, gain, shift, w_up, b_up, w_down, seq_len):
    width = rows.shape[1]
    units = w_up.shape[1]
    heads_width = att_mine.shape[1]
    step = min(seq_len, 256)
    steps = seq_len // step
    whole = lambda *shape: pl.BlockSpec(shape, lambda i, s: (0,) * len(shape))
    local = lambda n: pl.BlockSpec((step, n), lambda i, s: (i, 0))
    chosen = lambda n: pl.BlockSpec((step, n), lambda i, s: (s[0] * steps + i, 0))
    return pl.pallas_call(
        feed_forward_kernel,
        out_shape=(
            jax.ShapeDtypeStruct((seq_len, width), F32),
            jax.ShapeDtypeStruct((seq_len, width), BF16),
            jax.ShapeDtypeStruct((seq_len, units), BF16),
            jax.ShapeDtypeStruct((seq_len, units), BF16),
            jax.ShapeDtypeStruct((seq_len, width), F32),
            jax.ShapeDtypeStruct((seq_len, width), F32),
            jax.ShapeDtypeStruct((1, units), F32),
        ),
        grid_spec=pltpu.PrefetchScalarGridSpec(
            num_scalar_prefetch=1,
            grid=(steps,),
            in_specs=[
                chosen(width),
                chosen(width),
                local(heads_width),
                local(heads_width),
                whole(heads_width, width),
                whole(heads_width, width),
                whole(1, width),
                whole(1, width),
                whole(1, width),
                whole(width, units),
                whole(1, units),
                whole(units, width),
            ],
            out_specs=[
                local(width), local(width), local(units), local(units), local(width), local(width), whole(1, units),
            ],
        ),
        compiler_params=pltpu.CompilerParams(vmem_limit_bytes=VMEM_BYTES),
        cost_estimate=pl.CostEstimate(
            flops=2 * seq_len * width * (4 * units + 2 * heads_width),
            bytes_accessed=4 * units * width + 22 * seq_len * width,
            transcendentals=seq_len * units,
        ),
        name="feed_forward",
    )(seq, rows, cot, att_mine, att_peer, wo_mine, wo_peer, b_out, gain, shift, w_up, b_up, w_down)


def middle_gradient_kernel(
    seq_ref, mine_ref, peer_ref, middle_ref, cot_ref, gain_ref, grad_middle_ref, sums_ref,
):
    grad_normed = mine_ref[...] + peer_ref[...]
    cot = cot_ref[...]
    xhat, inverse_deviation = standardize(middle_ref[...])
    grad_middle = cot + norm_pull(grad_normed, gain_ref[...], xhat, inverse_deviation)
    grad_middle_ref[...] = grad_middle

    def total(values):
        return jnp.sum(values, 0, keepdims=True)

    sums_ref[...] = jnp.concatenate(
        [total(grad_normed * xhat), total(grad_normed), total(grad_middle), total(cot)]
        + [jnp.zeros_like(gain_ref[...])] * 4,
        axis=0,
    )


def input_gradient_kernel(
    seq_ref, mine_ref, peer_ref, rows_ref, grad_middle_ref, gain_ref, grad_rows_ref, sums_ref,
):
    grad_normed = mine_ref[...] + peer_ref[...]
    xhat, inverse_deviation = standardize(rows_ref[...])
    grad_rows_ref[...] = grad_middle_ref[...] + norm_pull(grad_normed, gain_ref[...], xhat, inverse_deviation)

    def total(values):
        return jnp.sum(values, 0, keepdims=True)

    sums_ref[...] = jnp.concatenate(
        [total(grad_normed * xhat), total(grad_normed)] + [jnp.zeros_like(gain_ref[...])] * 6, axis=0
    )


def norm_gradient(kernel, seq, mine, peer, third, fourth, gain, chosen, seq_len, name):
    width = mine.shape[1]
    own = pl.BlockSpec((seq_len, width), lambda i, s: (0, 0))
    pick = pl.BlockSpec((seq_len, width), lambda i, s: (s[0], 0))
    return pl.pallas_call(
        kernel,
        out_shape=(jax.ShapeDtypeStruct((seq_len, width), F32), jax.ShapeDtypeStruct((8, width), F32)),
        grid_spec=pltpu.PrefetchScalarGridSpec(
            num_scalar_prefetch=1,
            grid=(1,),
            in_specs=[own, own, pick if chosen == 2 else own, pick if chosen == 3 else own,
                      pl.BlockSpec((1, width), lambda i, s: (0, 0))],
            out_specs=[own, pl.BlockSpec((8, width), lambda i, s: (0, 0))],
        ),
        compiler_params=pltpu.CompilerParams(vmem_limit_bytes=VMEM_BYTES),
        cost_estimate=pl.CostEstimate(flops=20 * seq_len * width, bytes_accessed=20 * seq_len * width, transcendentals=seq_len),
        name=name,
    )(seq, mine, peer, third, fourth, gain)


def attention_backward_kernel(
    seq_ref, lengths_ref, grad_middle_ref, qkv_ref, lse_ref, w_out_ref, w_ref,
    grad_qkv_ref, grad_normed_ref, sums_ref, bias_ref, grad_att_ref,
):
    seq_len = grad_middle_ref.shape[0]
    width = w_ref.shape[2]
    grad_att_ref[...] = dot_bt(grad_middle_ref[...].astype(BF16), w_out_ref[...]).astype(BF16)
    bias_ref[...] = segment_bias(lengths_ref, seq_ref[0], seq_len)
    scale = 1.0 / math.sqrt(HEAD_DIM)
    for pair in range(width // LANES):
        cols = slice(pair * LANES, (pair + 1) * LANES)
        query, key, value = qkv_ref[0, :, cols], qkv_ref[1, :, cols], qkv_ref[2, :, cols]
        grad_att = grad_att_ref[:, cols]
        grad_query = grad_key = grad_value = 0.0
        for half in range(2):
            head = 2 * pair + half
            key_half = head_only(key, half)
            scores = dot_bt(key_half, query) + bias_ref[...]
            probs = jnp.exp(scores - lse_ref[head : head + 1, :])
            grad_probs = dot_bt(head_only(value, half), grad_att)
            inner = jnp.sum(grad_probs * probs, 0, keepdims=True)
            grad_scores = (probs * (grad_probs - inner)).astype(BF16)
            grad_value += dot(probs.astype(BF16), head_only(grad_att, half))
            grad_key += dot(grad_scores, head_only(query, half))
            grad_query += dot_at(grad_scores, key_half)
        grad_qkv_ref[0, :, cols] = (grad_query * scale).astype(BF16)
        grad_qkv_ref[1, :, cols] = grad_key.astype(BF16)
        grad_qkv_ref[2, :, cols] = grad_value.astype(BF16)
    grad_normed_ref[...] = (
        dot_bt(grad_qkv_ref[0], w_ref[0]) + dot_bt(grad_qkv_ref[1], w_ref[1]) + dot_bt(grad_qkv_ref[2], w_ref[2])
    )
    sums_ref[...] = jnp.concatenate(
        [jnp.sum(grad_qkv_ref[0].astype(F32), 0, keepdims=True), jnp.sum(grad_qkv_ref[2].astype(F32), 0, keepdims=True)]
        + [jnp.zeros((6, width), F32)],
        axis=0,
    )


def attention_backward(seq, lengths, grad_middle, qkv, lse, w_out, w_heads):
    seq_len, width = grad_middle.shape
    heads_width = w_heads.shape[2]
    whole = lambda *shape: pl.BlockSpec(shape, lambda i, s, n: (0,) * len(shape))
    return pl.pallas_call(
        attention_backward_kernel,
        out_shape=(
            jax.ShapeDtypeStruct((3, seq_len, heads_width), BF16),
            jax.ShapeDtypeStruct((seq_len, width), F32),
            jax.ShapeDtypeStruct((8, heads_width), F32),
        ),
        grid_spec=pltpu.PrefetchScalarGridSpec(
            num_scalar_prefetch=2,
            grid=(1,),
            in_specs=[
                whole(seq_len, width),
                whole(3, seq_len, heads_width),
                whole(*lse.shape),
                whole(heads_width, width),
                whole(3, width, heads_width),
            ],
            out_specs=[whole(3, seq_len, heads_width), whole(seq_len, width), whole(8, heads_width)],
            scratch_shapes=[pltpu.VMEM((seq_len, seq_len), F32), pltpu.VMEM((seq_len, heads_width), BF16)],
        ),
        compiler_params=pltpu.CompilerParams(vmem_limit_bytes=VMEM_BYTES),
        cost_estimate=pl.CostEstimate(
            flops=2 * seq_len * heads_width * (4 * width + 20 * seq_len),
            bytes_accessed=8 * seq_len * width + 8 * width * heads_width,
            transcendentals=seq_len * seq_len * heads_width // HEAD_DIM,
        ),
        name="attention_backward",
    )(seq, lengths, grad_middle, qkv, lse, w_out, w_heads)


def swap(values):
    return lax.ppermute(values, "tensor", [(0, 1), (1, 0)])


def exchange(values, stride, count):
    return lax.ppermute(values, "dp", [(i, i ^ stride) for i in range(count)])


def sum_over_dp(part, place, count):
    strides = [1 << i for i in range(count.bit_length() - 1)]
    taken = []
    for stride in strides:
        half = part.shape[0] // 2
        if stride != strides[-1] and part.shape[0] % 32 == 0:
            bit = (place // stride) % 2
            sent = lax.dynamic_slice_in_dim(part, (1 - bit) * half, half, 0)
            kept = lax.dynamic_slice_in_dim(part, bit * half, half, 0)
            part = kept + exchange(sent, stride, count)
            taken.append((stride, bit))
        else:
            part = part + exchange(part, stride, count)
    for stride, bit in reversed(taken):
        got = exchange(part, stride, count)
        size = part.shape[0]
        both = jnp.zeros((2 * size,) + part.shape[1:], part.dtype)
        both = lax.dynamic_update_slice_in_dim(both, part, bit * size, 0)
        part = lax.dynamic_update_slice_in_dim(both, got, (1 - bit) * size, 0)
    return part


def shards(dp_count, inputs, pair_lengths, first_norm_gain, first_norm_bias, w_qkv, b_qv, w_out, b_out,
           second_norm_gain, second_norm_bias, w_up, b_up, w_down, b_down, cotangent):
    seq_count = pair_lengths.shape[0]
    token_count, width = inputs.shape
    seq_len = token_count // seq_count
    heads_width = w_qkv.shape[2]
    units = w_up.shape[1]
    side = lax.axis_index("tensor")
    place = lax.axis_index("dp")
    own, other = side.astype(jnp.int32).reshape(1), (1 - side).astype(jnp.int32).reshape(1)
    w_heads = w_qkv.transpose(1, 0, 2)
    gain_one, shift_one = first_norm_gain.reshape(1, width), first_norm_bias.reshape(1, width)
    gain_two, shift_two = second_norm_gain.reshape(1, width), second_norm_bias.reshape(1, width)
    b_out_row, b_up_row = b_out.reshape(1, width), b_up.reshape(1, units)

    core = place % 2
    piece_rows = heads_width // 2
    piece = lax.dynamic_slice_in_dim(w_out, core * piece_rows, piece_rows, 0).astype(F32)
    piece = swap(piece)
    piece_two = exchange(piece, 1, dp_count)
    wo_peer = jnp.where(core == 0, jnp.concatenate([piece, piece_two]), jnp.concatenate([piece_two, piece]))

    def forward(seq):
        return attention_forward(seq, pair_lengths, inputs, w_heads, b_qv, gain_one, shift_one, seq_len)

    normed_own, qkv_own, att_own, lse_own = forward(own)
    att_peer_other = swap(att_own)
    normed_other, qkv_other, att_other, lse_other = forward(other)
    att_peer_own = swap(att_other)

    def feed(seq, att_mine, att_peer):
        return feed_forward(seq, inputs, cotangent, att_mine, att_peer, w_out, wo_peer, b_out_row, gain_two, shift_two,
                            w_up, b_up_row, w_down, seq_len)

    _, normed_two_other, hidden_other, grad_pre_other, down_other, gn_two_other, b_up_other = feed(other, att_other, att_peer_other)
    gn_two_peer = swap(gn_two_other)
    middle, normed_two_own, hidden_own, grad_pre_own, down_own, gn_two_own, b_up_own = feed(own, att_own, att_peer_own)

    rows_of = lambda values, seq: lax.dynamic_slice_in_dim(values, seq[0] * seq_len, seq_len, 0)
    cot_own, cot_other = rows_of(cotangent, own).astype(BF16), rows_of(cotangent, other).astype(BF16)
    grad_w_down = dot_at(hidden_own, cot_own) + dot_at(hidden_other, cot_other)
    grad_w_up = dot_at(normed_two_own, grad_pre_own) + dot_at(normed_two_other, grad_pre_other)
    grad_w_down = sum_over_dp(grad_w_down, place, dp_count)
    grad_w_up = sum_over_dp(grad_w_up, place, dp_count)

    grad_middle_own, sums_two = norm_gradient(
        middle_gradient_kernel, own, gn_two_own, gn_two_peer, middle, cotangent, gain_two, 3, seq_len, "middle_gradient")
    grad_middle_other = swap(grad_middle_own)

    def backward(seq, grad_middle, qkv, lse):
        return attention_backward(seq, pair_lengths, grad_middle, qkv, lse, w_out, w_heads)

    grad_qkv_own, gn_one_own, b_qv_own = backward(own, grad_middle_own, qkv_own, lse_own)
    grad_qkv_other, gn_one_other, b_qv_other = backward(other, grad_middle_other, qkv_other, lse_other)
    gn_one_peer = swap(gn_one_other)
    grad_w_out = dot_at(att_own.astype(BF16), grad_middle_own.astype(BF16)) + dot_at(
        att_other.astype(BF16), grad_middle_other.astype(BF16))
    grad_w_heads = jnp.concatenate(
        [dot_at(normed_own, grad_qkv_own[j]) + dot_at(normed_other, grad_qkv_other[j]) for j in range(3)])
    grad_w_out = sum_over_dp(grad_w_out, place, dp_count)
    grad_w_heads = sum_over_dp(grad_w_heads, place, dp_count)

    grad_inputs_own, sums_one = norm_gradient(
        input_gradient_kernel, own, gn_one_own, gn_one_peer, inputs, grad_middle_own, gain_one, 2, seq_len, "input_gradient")
    grad_inputs_other = swap(grad_inputs_own)

    down_peer = swap(down_other)
    output_own = middle + (down_own + down_peer) + b_down
    output_other = swap(output_own)

    def whole_rows(mine, peer):
        both = jnp.zeros((token_count, width), F32)
        both = lax.dynamic_update_slice_in_dim(both, mine, own[0] * seq_len, 0)
        return lax.dynamic_update_slice_in_dim(both, peer, other[0] * seq_len, 0)

    sums = jnp.concatenate([sums_two[:4], sums_one[:2]])
    sums = sums + swap(sums)
    b_qv_sum = (b_qv_own + b_qv_other)[:2]
    wide = max(width, units, 2 * heads_width)
    row = lambda values: jnp.pad(values.reshape(1, -1), ((0, 0), (0, wide - values.size)))
    small = jnp.concatenate([row(sums[i]) for i in range(6)] + [row(b_up_own + b_up_other), row(b_qv_sum)])
    small = sum_over_dp(small, place, dp_count)
    return (
        whole_rows(output_own, output_other),
        whole_rows(grad_inputs_own, grad_inputs_other),
        small[4, :width],
        small[5, :width],
        grad_w_heads.reshape(3, width, heads_width).transpose(1, 0, 2),
        small[7, : 2 * heads_width].reshape(2, heads_width),
        grad_w_out,
        small[2, :width],
        small[0, :width],
        small[1, :width],
        grad_w_up,
        small[6, :units],
        grad_w_down,
        small[3, :width],
    )


def solution(mesh):
    rows, copied, columns = P("dp", None), P(), P(None, "tensor")
    heads, split_rows = P(None, None, "tensor"), P("tensor", None)
    return jax.shard_map(
        functools.partial(shards, mesh.shape["dp"]),
        mesh=mesh,
        in_specs=(rows, rows, copied, copied, heads, columns, split_rows, copied, copied, copied, columns,
                  P("tensor"), split_rows, copied, rows),
        out_specs=(rows, rows, copied, copied, heads, columns, split_rows, copied, copied, copied, columns,
                   P("tensor"), split_rows, copied),
        check_vma=False,
    )
```

```python
import functools
import math
import types

import jax
import jax.numpy as jnp
from jax import lax
from jax.experimental import pallas as pl
from jax.experimental.pallas import tpu as pltpu
from jax.sharding import PartitionSpec as P

HEAD_DIM = 64
LANES = 128
EPS = 1e-06
MASKED = -1e30
MIB = 1024 * 1024
F32 = jnp.float32
BF16 = jnp.bfloat16
ERFC_P = 0.3925
ERFC_C = (
    0.2342248384381894,
    0.1104885068031651,
    0.6008554065531575,
    -0.5658356357906557,
    0.8411781949001069,
    -0.22091131771921121,
)


def dot(left, right):
    return lax.dot_general(left, right, (((1,), (0,)), ((), ())), preferred_element_type=F32)


def dot_bt(left, right):
    return lax.dot_general(left, right, (((1,), (1,)), ((), ())), preferred_element_type=F32)


def dot_at(left, right):
    return lax.dot_general(left, right, (((0,), (0,)), ((), ())), preferred_element_type=F32)


def standardize(values):
    row_mean = jnp.mean(values, -1, keepdims=True)
    centred = values - row_mean
    inverse_deviation = lax.rsqrt(jnp.mean(centred * centred, -1, keepdims=True) + EPS)
    return centred * inverse_deviation, inverse_deviation


def norm_pull(grad_normed, gain, xhat, inverse_deviation):
    scaled = grad_normed * gain
    return inverse_deviation * (
        scaled
        - jnp.mean(scaled, -1, keepdims=True)
        - xhat * jnp.mean(scaled * xhat, -1, keepdims=True)
    )


def segment_bias(lengths_ref, seq, seq_len):
    end_one = lengths_ref[seq, 0]
    end_two = end_one + lengths_ref[seq, 1]
    end_three = end_two + lengths_ref[seq, 2]

    def ids(shape, dim):
        place = lax.broadcasted_iota(jnp.int32, shape, dim)
        return (
            (place >= end_one).astype(jnp.int32)
            + (place >= end_two).astype(jnp.int32)
            + (place >= end_three).astype(jnp.int32)
        )

    same = ids((seq_len, seq_len), 0) == ids((seq_len, seq_len), 1)
    return jnp.where(same, 0.0, MASKED).astype(F32)


def head_only(block, half):
    lane = lax.broadcasted_iota(jnp.int32, block.shape, 1)
    mine = (lane < HEAD_DIM) if half == 0 else (lane >= HEAD_DIM)
    return jnp.where(mine, block, jnp.zeros_like(block))


ANY = pl.BlockSpec(memory_space=pl.ANY)


def call(kernel, name, grid, inputs, outputs, vmem_mib, flops, prefetch=(), scratch=(), after=(), aliases=None):
    arrays, in_specs = [a for a, _ in inputs], [b for _, b in inputs]
    first = len(prefetch) + len(arrays)

    def body(*refs):
        kernel(*refs[:first], *refs[first + len(after) :])

    return pl.pallas_call(
        body,
        out_shape=tuple(jax.ShapeDtypeStruct(shape, dtype) for shape, dtype, _ in outputs),
        grid_spec=pltpu.PrefetchScalarGridSpec(
            num_scalar_prefetch=len(prefetch),
            grid=grid,
            in_specs=in_specs + [ANY] * len(after),
            out_specs=tuple(spec for _, _, spec in outputs),
            scratch_shapes=list(scratch),
        ),
        input_output_aliases=aliases or {},
        compiler_params=pltpu.CompilerParams(vmem_limit_bytes=vmem_mib * MIB),
        cost_estimate=pl.CostEstimate(flops=1, bytes_accessed=1, transcendentals=0),
        name=name,
    )(*prefetch, *arrays, *after)


def whole(array):
    shape = array if isinstance(array, tuple) else array.shape
    return pl.BlockSpec(shape, lambda *_: (0,) * len(shape))


def at_sequence(rows, columns):
    return pl.BlockSpec((rows, columns), lambda i, seq, *_: (seq[0], 0))


def attention_forward_kernel(
    seq_ref, lengths_ref, rows_ref, w_ref, b_ref, gain_ref, shift_ref,
    normed_ref, qkv_ref, attended_ref, lse_ref, bias_ref,
):
    seq_len = rows_ref.shape[0]
    width = w_ref.shape[2]
    xhat, _ = standardize(rows_ref[...])
    normed = (xhat * gain_ref[...] + shift_ref[...]).astype(BF16)
    normed_ref[...] = normed
    scale = 1.0 / math.sqrt(HEAD_DIM)
    qkv_ref[0] = ((dot(normed, w_ref[0]) + b_ref[0:1]).astype(BF16).astype(F32) * scale).astype(BF16)
    qkv_ref[1] = dot(normed, w_ref[1]).astype(BF16)
    qkv_ref[2] = (dot(normed, w_ref[2]) + b_ref[1:2]).astype(BF16)
    bias_ref[...] = segment_bias(lengths_ref, seq_ref[0], seq_len)
    lane = lax.broadcasted_iota(jnp.int32, (seq_len, LANES), 1)
    stats = jnp.zeros((seq_len, LANES), F32)
    for pair in range(width // LANES):
        cols = slice(pair * LANES, (pair + 1) * LANES)
        query, key, value = qkv_ref[0, :, cols], qkv_ref[1, :, cols], qkv_ref[2, :, cols]
        mixed = None
        for half in range(2):
            scores = dot_bt(query, head_only(key, half)) + bias_ref[...]
            row_max = jnp.max(scores, -1, keepdims=True)
            exps = jnp.exp(scores - row_max)
            total = jnp.sum(exps, -1, keepdims=True)
            probs = (exps * (1.0 / total)).astype(BF16)
            part = dot(probs, head_only(value, half))
            mixed = part if mixed is None else mixed + part
            stats = jnp.where(lane == 2 * pair + half, row_max + jnp.log(total), stats)
        attended_ref[:, cols] = mixed.astype(BF16).astype(F32)
    lse_ref[...] = stats.T[: lse_ref.shape[0]]


def feed_forward_kernel(
    seq_ref, rows_ref, cot_ref, att_mine_ref, att_peer_ref, wo_mine_ref, wo_peer_ref, b_out_ref,
    gain_ref, shift_ref, w_up_ref, b_up_ref, w_down_ref,
    middle_ref, normed_ref, hidden_ref, grad_pre_ref, down_ref, grad_normed_low, grad_normed_high, grad_b_up_ref,
):
    middle = (
        rows_ref[...]
        + dot(att_mine_ref[...].astype(BF16), wo_mine_ref[...])
        + dot(att_peer_ref[...].astype(BF16), wo_peer_ref[...].astype(BF16))
        + b_out_ref[...]
    )
    middle_ref[...] = middle
    xhat, _ = standardize(middle)
    normed = (xhat * gain_ref[...] + shift_ref[...]).astype(BF16)
    normed_ref[...] = normed
    cot = cot_ref[...].astype(BF16)

    @pl.when(pl.program_id(0) == 0)
    def _():
        grad_b_up_ref[...] = jnp.zeros_like(grad_b_up_ref)

    pre = dot(normed, w_up_ref[...]) + b_up_ref[...]
    size = jnp.abs(pre) * math.sqrt(0.5)
    t = 1.0 / (1.0 + ERFC_P * size)
    gauss = jnp.exp(-0.5 * (pre * pre))
    poly = ERFC_C[-1]
    for c in ERFC_C[-2::-1]:
        poly = poly * t + c
    tail = 0.5 * (poly * t) * gauss
    cdf = jnp.where(pre >= 0, 1.0 - tail, tail)
    hidden = (pre * cdf).astype(BF16)
    slope = cdf + pre * gauss * (1.0 / math.sqrt(2.0 * math.pi))
    hidden_ref[...] = hidden
    down_ref[...] = dot(hidden, w_down_ref[...])
    grad_pre = (dot_bt(cot, w_down_ref[...]) * slope).astype(BF16)
    grad_pre_ref[...] = grad_pre
    grad_b_up_ref[...] += jnp.sum(grad_pre.astype(F32), 0, keepdims=True)
    grad_normed = dot_bt(grad_pre, w_up_ref[...])

    @pl.when(pl.program_id(0) == 0)
    def _():
        grad_normed_low[...] = grad_normed

    @pl.when(pl.program_id(0) == 1)
    def _():
        grad_normed_high[...] = grad_normed


def middle_gradient_kernel(
    seq_ref, mine_ref, peer_ref, middle_ref, cot_ref, gain_ref, grad_middle_ref, sums_ref,
):
    grad_normed = mine_ref[...] + peer_ref[...]
    cot = cot_ref[...]
    xhat, inverse_deviation = standardize(middle_ref[...])
    grad_middle = cot + norm_pull(grad_normed, gain_ref[...], xhat, inverse_deviation)
    grad_middle_ref[...] = grad_middle

    def total(values):
        return jnp.sum(values, 0, keepdims=True)

    sums_ref[...] = jnp.concatenate(
        [total(grad_normed * xhat), total(grad_normed), total(grad_middle), total(cot)]
        + [jnp.zeros((4, cot.shape[1]), F32)],
        axis=0,
    )


def input_gradient_kernel(
    seq_ref, mine_ref, peer_ref, rows_ref, middle_low, middle_high, gain_ref, grad_rows_ref, sums_ref,
):
    grad_normed = mine_ref[...] + peer_ref[...]
    xhat, inverse_deviation = standardize(rows_ref[...])
    pulled = norm_pull(grad_normed, gain_ref[...], xhat, inverse_deviation)
    half = middle_low.shape[0]
    grad_rows_ref[0:half] = middle_low[...] + pulled[0:half]
    grad_rows_ref[half:] = middle_high[...] + pulled[half:]

    def total(values):
        return jnp.sum(values, 0, keepdims=True)

    sums_ref[...] = jnp.concatenate(
        [total(grad_normed * xhat), total(grad_normed), jnp.zeros((6, xhat.shape[1]), F32)], axis=0
    )


def attention_backward_kernel(
    seq_ref, lengths_ref, middle_low, middle_high, qkv_ref, lse_ref, w_out_ref, w_ref,
    grad_qkv_ref, grad_normed_ref, sums_ref, bias_ref, grad_att_ref,
):
    seq_len, width = grad_att_ref.shape
    half = middle_low.shape[0]
    grad_att_ref[0:half] = dot_bt(middle_low[...].astype(BF16), w_out_ref[...]).astype(BF16)
    grad_att_ref[half:] = dot_bt(middle_high[...].astype(BF16), w_out_ref[...]).astype(BF16)
    bias_ref[...] = segment_bias(lengths_ref, seq_ref[0], seq_len)
    scale = 1.0 / math.sqrt(HEAD_DIM)
    for pair in range(width // LANES):
        cols = slice(pair * LANES, (pair + 1) * LANES)
        query, key, value = qkv_ref[0, :, cols], qkv_ref[1, :, cols], qkv_ref[2, :, cols]
        grad_att = grad_att_ref[:, cols]
        grad_query = grad_key = grad_value = 0.0
        for half in range(2):
            head = 2 * pair + half
            key_half = head_only(key, half)
            scores = dot_bt(key_half, query) + bias_ref[...]
            probs = jnp.exp(scores - lse_ref[head : head + 1, :])
            grad_probs = dot_bt(head_only(value, half), grad_att)
            inner = jnp.sum(grad_probs * probs, 0, keepdims=True)
            grad_scores = (probs * (grad_probs - inner)).astype(BF16)
            grad_value += dot(probs.astype(BF16), head_only(grad_att, half))
            grad_key += dot(grad_scores, head_only(query, half))
            grad_query += dot_at(grad_scores, key_half)
        grad_qkv_ref[0, :, cols] = (grad_query * scale).astype(BF16)
        grad_qkv_ref[1, :, cols] = grad_key.astype(BF16)
        grad_qkv_ref[2, :, cols] = grad_value.astype(BF16)
    grad_normed_ref[...] = (
        dot_bt(grad_qkv_ref[0], w_ref[0]) + dot_bt(grad_qkv_ref[1], w_ref[1]) + dot_bt(grad_qkv_ref[2], w_ref[2])
    )
    sums_ref[...] = jnp.concatenate(
        [jnp.sum(grad_qkv_ref[0].astype(F32), 0, keepdims=True), jnp.sum(grad_qkv_ref[2].astype(F32), 0, keepdims=True)]
        + [jnp.zeros((6, width), F32)],
        axis=0,
    )


def attention_forward(seq, lengths, rows, w_heads, b_qv, gain, shift, seq_len, after=()):
    width, heads_width = rows.shape[1], w_heads.shape[2]
    stat_rows = 8 * pl.cdiv(heads_width // HEAD_DIM, 8)
    shapes = [((seq_len, width), BF16), ((3, seq_len, heads_width), BF16), ((seq_len, heads_width), F32), ((stat_rows, seq_len), F32)]
    return call(
        attention_forward_kernel, "attention_forward", (1,),
        [(rows, at_sequence(seq_len, width))] + [(a, whole(a)) for a in (w_heads, b_qv, gain, shift)],
        [(shape, dtype, whole(shape)) for shape, dtype in shapes],
        28, 2 * seq_len * heads_width * (3 * width + 8 * seq_len),
        prefetch=(seq, lengths), scratch=[pltpu.VMEM((seq_len, seq_len), F32)], after=after,
    )


def feed_forward(seq, rows, cot, att_mine, att_peer, wo_mine, wo_peer, b_out, gain, shift, w_up, b_up, w_down, seq_len, after=()):
    width, units = w_up.shape
    heads_width = att_mine.shape[1]
    steps = 2
    step = seq_len // steps
    local = lambda n: pl.BlockSpec((step, n), lambda i, s: (i, 0))
    chosen = pl.BlockSpec((step, width), lambda i, s: (s[0] * steps + i, 0))
    made = lambda n, dtype: ((seq_len, n), dtype, local(n))
    return call(
        feed_forward_kernel, "feed_forward", (steps,),
        [(rows, chosen), (cot, chosen), (att_mine, local(heads_width)), (att_peer, local(heads_width))]
        + [(a, whole(a)) for a in (wo_mine, wo_peer, b_out, gain, shift, w_up, b_up, w_down)],
        [made(width, F32), made(width, BF16), made(units, BF16), made(units, BF16), made(width, F32),
         piece_spec((step, width)), piece_spec((step, width)), ((1, units), F32, whole((1, units)))],
        44, 2 * seq_len * width * (4 * units + 2 * heads_width),
        prefetch=(seq,), after=after,
    )


def middle_gradient(blocks, mine, peer, middle, cotangent, gain, after=()):
    rows, width = mine.shape
    picked = lambda n: pl.BlockSpec((rows, width), lambda i, b: (b[n], 0))
    return call(
        middle_gradient_kernel, "middle_gradient", (1,),
        [(mine, whole(mine)), (peer, whole(peer)), (middle, picked(0)), (cotangent, picked(1)), (gain, whole(gain))],
        [piece_spec((rows, width)), piece_spec((8, width))],
        28, 20 * rows * width, prefetch=(blocks,), after=after,
    )


def input_gradient(seq, mine, peer, inputs, middles, gain, after=()):
    rows, width = mine.shape
    return call(
        input_gradient_kernel, "input_gradient", (1,),
        [(mine, whole(mine)), (peer, whole(peer)), (inputs, at_sequence(rows, width))] + [(a, whole(a)) for a in (*middles, gain)],
        [piece_spec((rows, width)), piece_spec((8, width))],
        28, 20 * rows * width, prefetch=(seq,), after=after,
    )


def attention_backward(seq, lengths, middles, qkv, lse, w_out, w_heads, after=()):
    seq_len, width = qkv.shape[1], w_out.shape[1]
    heads_width = w_heads.shape[2]
    return call(
        attention_backward_kernel, "attention_backward", (1,),
        [(a, whole(a)) for a in (*middles, qkv, lse, w_out, w_heads)],
        [(shape, dtype, whole(shape)) for shape, dtype in
         (((3, seq_len, heads_width), BF16), ((seq_len, width), F32), ((8, heads_width), F32))],
        34, 2 * seq_len * heads_width * (4 * width + 20 * seq_len),
        prefetch=(seq, lengths), after=after,
        scratch=[pltpu.VMEM((seq_len, seq_len), F32), pltpu.VMEM((seq_len, heads_width), BF16)],
    )


def swap(values):
    return lax.ppermute(values, "tensor", [(0, 1), (1, 0)])


def exchange(values, stride, count):
    return lax.ppermute(values, "dp", [(i, i ^ stride) for i in range(count)])


def piece_spec(shape):
    return shape, F32, whole(shape)


def quarter_start(bits_ref, kept, dy, dz, quarter):
    core, y, z = bits_ref[0], bits_ref[1], bits_ref[2]
    core = core if kept else 1 - core
    return ((core * 2 + (1 - y if dy else y)) * 2 + (1 - z if dz else z)) * quarter


def quarters(kept):
    return [(kept, dy, dz) for dy, dz in ((1, 1), (1, 0), (0, 1), (0, 0))]


def put_pieces(bits_ref, half_ref, kept, pieces):
    quarter = half_ref.shape[0] // 4
    y, z = bits_ref[1], bits_ref[2]
    each = len(pieces) // 4
    for k, (_, dy, dz) in enumerate(quarters(kept)):
        start = ((1 - y if dy else y) * 2 + (1 - z if dz else z)) * quarter
        for sub in range(each):
            size = quarter // each
            pieces[k * each + sub][...] = half_ref[pl.ds(pl.multiple_of(start + sub * size, 8), size)]


def weight_gradient_kernel(bits_ref, side_ref, left_own, left_other, right_own, right_other, *refs):
    pieces, half_ref = refs[:-1], refs[-1]
    own, other = right_own[...].astype(BF16), right_other[...].astype(BF16)
    rows = half_ref.shape[0]
    for kept in range(2):
        core = bits_ref[0] if kept else 1 - bits_ref[0]
        cols = pl.ds(pl.multiple_of(core * rows, LANES), rows)
        half_ref[...] = dot_at(left_own[:, cols], own) + dot_at(left_other[:, cols], other)
        put_pieces(bits_ref, half_ref, kept, pieces[-4:] if kept else pieces[:-4])


SUB = 1


def piece_outputs(rows, columns):
    return [piece_spec((rows // 8 // SUB, columns))] * (4 * SUB) + [piece_spec((rows // 8, columns))] * 4


def weight_gradient(bits, side, lefts, rights, seq_len, name, after=()):
    pair = isinstance(rights, tuple)
    own, other = rights if pair else (rights, rights)
    rows, columns = lefts[0].shape[1], own.shape[1]
    left = whole(lefts[0])
    right_own = pl.BlockSpec((seq_len, columns), lambda i, b, s: (0 if pair else s[0], 0))
    right_other = pl.BlockSpec((seq_len, columns), lambda i, b, s: (0 if pair else 1 - s[0], 0))
    made = call(
        weight_gradient_kernel, name, (1,),
        [(lefts[0], left), (lefts[1], left), (own, right_own), (other, right_other)],
        piece_outputs(rows, columns), 40, 4 * seq_len * rows * columns, prefetch=(bits, side), after=after,
        scratch=[pltpu.VMEM((rows // 2, columns), F32)],
    )
    return made[:-4], made[-4:]


def attention_weight_gradients_kernel(
    bits_ref, normed_own, normed_other, qkv_own, qkv_other, att_own, att_other, own_low, own_high, other_low, other_high, *pieces,
):
    side = pieces[-1].shape[0]
    low, high = slice(0, own_low.shape[0]), slice(own_low.shape[0], None)
    out_terms = ((att_own, low, own_low), (att_own, high, own_high), (att_other, low, other_low), (att_other, high, other_high))
    for kept in range(2):
        for k, which in enumerate(quarters(kept)):
            targets = pieces[-4 + k :][:1] if kept else pieces[k * SUB : (k + 1) * SUB]
            block = quarter_start(bits_ref, *which, 1)
            cols = pl.ds(pl.multiple_of((block % 2) * side, LANES), side)

            def put(value):
                size = targets[0].shape[0]
                for sub, target in enumerate(targets):
                    target[...] = value[sub * size : (sub + 1) * size]

            @pl.when(block < 6)
            def _():
                j = jnp.minimum(block // 2, 2)
                put(dot_at(normed_own[:, cols], qkv_own[j]) + dot_at(normed_other[:, cols], qkv_other[j]))

            @pl.when(block >= 6)
            def _():
                put(sum(dot_at(att[rows].astype(BF16), middle[:, cols].astype(BF16)) for att, rows, middle in out_terms))


def attention_weight_gradients(bits, normeds, qkvs, atts, middles, after=()):
    seq_len, side = atts[0].shape
    made = call(
        attention_weight_gradients_kernel, "attention_weight_gradients", (1,),
        [(a, whole(a)) for a in (*normeds, *qkvs, *atts, *middles)],
        piece_outputs(8 * side, side), 40, 32 * seq_len * side * side, prefetch=(bits,), after=after,
    )
    return made[:-4], made[-4:]


def first_add_kernel(*refs):
    kept, got, sums = refs[:4], refs[4:-4], refs[-4:]
    each = len(got) // 4
    for k in range(4):
        size = got[0].shape[0]
        for sub in range(each):
            rows = pl.ds(sub * size, size)
            sums[k][rows] = kept[k][rows] + got[k * each + sub][...]


def first_add(kept, got, after=()):
    arrays = (*kept, *got)
    return call(first_add_kernel, "first_add", (1,), [(a, whole(a)) for a in arrays], [piece_spec(a.shape) for a in kept],
                24, 1, after=after)


def add_kernel(count, *refs):
    sums = refs[count:]
    for k, ref in enumerate(sums):
        total = refs[k][...]
        for more in refs[k + len(sums) : count : len(sums)]:
            total = total + more[...]
        ref[...] = total


def add(outs, *arrays, after=()):
    made = call(functools.partial(add_kernel, len(arrays)), "add", (1,), [(a, whole(a)) for a in arrays],
                [piece_spec(arrays[k].shape) for k in range(outs)], 24, 1, after=after)
    return made if outs > 1 else made[0]


def place_kernel(at, count, prefetched_ref, *refs):
    outs, sems = refs[count:-1], refs[-1]
    copies = []
    for k in range(count):
        where = at(prefetched_ref, k)
        for wanted, target, place in where:
            copy = pltpu.make_async_copy(refs[k], outs[target].at[place], sems.at[k])
            if wanted is None:
                copy.start()
            else:
                pl.when(wanted)(copy.start)
    for k in range(count):
        for wanted, target, place in at(prefetched_ref, k):
            copy = pltpu.make_async_copy(refs[k], outs[target].at[place], sems.at[k])
            if wanted is None:
                copy.wait()
            else:
                pl.when(wanted)(copy.wait)


def place_pieces(at, numbers, pieces, shapes, after=()):
    return call(
        functools.partial(place_kernel, at, len(pieces)), "place_pieces", (1,), [(p, whole(p)) for p in pieces],
        [(shape, F32, ANY) for shape in shapes], 24, 0, prefetch=(numbers,),
        scratch=[pltpu.SemaphoreType.DMA((len(pieces),))], after=after,
    )


def piece_number(bits_ref, k):
    core, y, z = bits_ref[0], bits_ref[1], bits_ref[2]
    flip = lambda bit, on: 1 - bit if on else bit
    return (flip(core, k & 4) * 2 + flip(y, k & 2)) * 2 + flip(z, k & 1)


def place_rows(bits, pieces, after=()):
    rows, columns = pieces[0].shape

    def at(bits_ref, k):
        return [(None, 0, pl.ds(pl.multiple_of(piece_number(bits_ref, k) * rows, 8), rows))]

    return place_pieces(at, bits, pieces, [(8 * rows, columns)], after)


def place_attention(bits, pieces, after=()):
    side = pieces[0].shape[0]

    def at(bits_ref, k):
        number = piece_number(bits_ref, k)
        return [
            (number < 6, 0, jnp.minimum(number, 5)),
            (number == 6, 1, (pl.ds(0, side), pl.ds(0, side))),
            (number == 7, 1, (pl.ds(0, side), pl.ds(side, side))),
        ]

    return place_pieces(at, bits, pieces, [(6, side, side), (side, 2 * side)], after)


def whole_rows(own, mine, peer, after=()):
    rows, columns = mine.shape

    def at(own_ref, k):
        which = own_ref[0] if k == 0 else 1 - own_ref[0]
        return [(None, 0, pl.ds(pl.multiple_of(which * rows, 8), rows))]

    return place_pieces(at, own, (mine, peer), [(2 * rows, columns)], after)[0]


def output_kernel(middle_ref, mine_ref, peer_ref, b_ref, output_ref):
    output_ref[...] = middle_ref[...] + (mine_ref[...] + peer_ref[...]) + b_ref[...]


def output_rows(middle, mine, peer, b_down, after=()):
    rows, width = middle.shape
    block = pl.BlockSpec((rows // 4, width), lambda i: (i, 0))
    return call(output_kernel, "output_rows", (4,), [(middle, block), (mine, block), (peer, block), (b_down, whole(b_down))],
                [(middle.shape, F32, block)], 16, 3 * middle.size, after=after)[0]


def gate(value, after):
    return call(lambda *refs: None, "gate", (1,), [(value, ANY)], [(value.shape, value.dtype, ANY)], 8, 0, after=after,
                aliases={0: 0})[0]


class DpSum:
    def __init__(self, count, halves):
        self.count = count
        self.kept = halves[1]
        self.flying = [exchange(piece, 1, count) for piece in halves[0]]

    def over_core(self, after=()):
        self.ya, self.yb, self.ka, self.kb = first_add(self.kept, self.flying, after)
        self.ya = exchange(self.ya, 2, self.count)
        self.yb = exchange(self.yb, 2, self.count)
        return self.kb

    def over_y(self, after=()):
        sent = add(1, self.ka, self.ya, after=after)
        self.flying = exchange(sent, 4, self.count)
        return sent

    def over_z(self, after=()):
        self.mine = add(1, self.kb, self.yb, self.flying, after=after)
        self.strides = [1 << i for i in range(3, self.count.bit_length() - 1)]
        self.flying = exchange(self.mine, self.strides.pop(0), self.count)
        return self.mine

    def total(self, after=()):
        self.mine = add(1, self.mine, self.flying, after=after)
        while self.strides:
            self.mine = add(1, self.mine, exchange(self.mine, self.strides.pop(0), self.count))
        self.held = [self.mine, exchange(self.mine, 4, self.count)]
        self.held += [exchange(self.mine, 2, self.count)]
        return self.mine

    def back_y(self, after=()):
        if after:
            self.held[1] = gate(self.held[1], after)
        self.held += [exchange(self.held[1], 2, self.count)]
        self.held += [exchange(self.held[k], 1, self.count) for k in range(2)]
        return self.held[1]

    def back_core(self, after=()):
        if after:
            self.held[2] = gate(self.held[2], after)
        self.held += [exchange(self.held[k], 1, self.count) for k in (2, 3)]
        return self.held[2]


def bundle_kernel(two_low, two_high, one_ref, sums_ref):
    two = two_low[0:4] + two_high[0:4]
    sums_ref[...] = jnp.concatenate([two, one_ref[0:2], jnp.zeros_like(one_ref[0:2])], axis=0)


def local_rows_kernel(mine_ref, peer_ref, up_own, up_other, qv_own, qv_other, sums_ref):
    width, side = mine_ref.shape[1], qv_own.shape[1]
    sums_ref[...] = jnp.zeros_like(sums_ref)
    sums_ref[0:8] = mine_ref[...] + peer_ref[...]
    up = up_own[...] + up_other[...]
    for j in range(up.shape[1] // width):
        sums_ref[8 + j : 9 + j] = up[:, j * width : (j + 1) * width]
    qv = qv_own[...] + qv_other[...]
    sums_ref[15:16, 0:side] = qv[0:1]
    sums_ref[15:16, side : 2 * side] = qv[1:2]


ORDER = (
    "FFo", "FFw*", "mda", "dWd", "dWu", "mdb", "Doc", "Doy*", "bwo", "Uoc", "bwt", "Doz", "Uoy*", "dn*", "dWa",
    "Aoc", "Uoz", "or*", "Dt", "Aoy", "Dby", "Aoz", "Ut", "Uby", "ig", "Dbc", "s0", "Ubc*", "At", "Aby*", "Abc",
    "op", "Dp", "s1", "s2", "Up", "s3", "s4", "Ap", "ip*",
)


def shards(dp_count, inputs, pair_lengths, first_norm_gain, first_norm_bias, w_qkv, b_qv, w_out, b_out,
           second_norm_gain, second_norm_bias, w_up, b_up, w_down, b_down, cotangent):
    seq_count = pair_lengths.shape[0]
    token_count, width = inputs.shape
    seq_len = token_count // seq_count
    heads_width = w_qkv.shape[2]
    units = w_up.shape[1]
    side = lax.axis_index("tensor")
    place = lax.axis_index("dp")
    own, other = side.astype(jnp.int32).reshape(1), (1 - side).astype(jnp.int32).reshape(1)
    core = place % 2
    bits = jnp.stack([core, (place // 2) % 2, (place // 4) % 2]).astype(jnp.int32)
    w_heads = w_qkv.transpose(1, 0, 2)
    row = lambda v: v
    gain_one, shift_one, gain_two, shift_two = map(row, (first_norm_gain, first_norm_bias, second_norm_gain, second_norm_bias))
    b_out_row, b_up_row, b_down_row = row(b_out), row(b_up), row(b_down)

    piece_rows = heads_width // 2
    piece = lax.dynamic_slice_in_dim(w_out, core * piece_rows, piece_rows, 0).astype(F32)
    piece = swap(piece)
    piece_two = exchange(piece, 1, dp_count)
    wo_peer = jnp.where(core == 0, jnp.concatenate([piece, piece_two]), jnp.concatenate([piece_two, piece]))

    def forward(seq, after=()):
        return attention_forward(seq, pair_lengths, inputs, w_heads, b_qv, gain_one, shift_one, seq_len, after)

    normed_own, qkv_own, att_own, lse_own = forward(own)
    att_peer_other = swap(att_own)
    normed_other, qkv_other, att_other, lse_other = forward(other, (att_own,))
    att_peer_own = swap(att_other)
    v = types.SimpleNamespace()

    def feed(seq, att_mine, att_peer, after=()):
        return feed_forward(seq, inputs, cotangent, att_mine, att_peer, w_out, wo_peer, b_out_row, gain_two, shift_two,
                            w_up, b_up_row, w_down, seq_len, after)

    def feed_other(after):
        _, v.normed_two_other, v.hidden_other, v.grad_pre_other, v.down_other, low, high, v.b_up_other = feed(
            other, att_other, att_peer_other)
        v.gn_two_peer = swap(low), swap(high)
        return v.hidden_other

    def feed_own(after):
        v.middle, v.normed_two_own, v.hidden_own, v.grad_pre_own, v.down_own, low, high, v.b_up_own = feed(
            own, att_own, att_peer_own, after)
        v.gn_two_own = low, high
        return v.hidden_own

    def down_product(after):
        v.down = DpSum(dp_count, weight_gradient(
            bits, own, (v.hidden_own, v.hidden_other), cotangent, seq_len, "down_weight_gradient", after))
        return v.down.kept[0]

    def up_product(after):
        v.up = DpSum(dp_count, weight_gradient(
            bits, own, (v.normed_two_own, v.normed_two_other), (v.grad_pre_own, v.grad_pre_other), seq_len,
            "up_weight_gradient", after))
        return v.up.kept[0]

    v.middles_own, v.middles_other, v.sums_two = [], [], []

    def middle_half(half, after):
        blocks = jnp.concatenate([own * 0 + half, own * 2 + half])
        made, sums = middle_gradient(
            blocks, v.gn_two_own[half], v.gn_two_peer[half], v.middle, cotangent, gain_two, after)
        v.middles_own.append(made)
        v.middles_other.append(swap(made))
        v.sums_two.append(sums)
        return made

    def backward(seq, middles, qkv, lse, after):
        return attention_backward(seq, pair_lengths, middles, qkv, lse, w_out, w_heads, after)

    def backward_own(after):
        v.grad_qkv_own, v.gn_one_own, v.b_qv_own = backward(own, v.middles_own, qkv_own, lse_own, after)
        return v.gn_one_own

    def send_down(after):
        v.down_peer = swap(gate(v.down_other, after))

    def backward_other(after):
        v.grad_qkv_other, v.gn_one_other, v.b_qv_other = backward(other, v.middles_other, qkv_other, lse_other, after)
        v.gn_one_peer = swap(v.gn_one_other)
        return v.gn_one_other

    def heads_product(after):
        v.heads = DpSum(dp_count, attention_weight_gradients(
            bits, (normed_own, normed_other), (v.grad_qkv_own, v.grad_qkv_other), (att_own, att_other),
            (*v.middles_own, *v.middles_other), after))
        return v.heads.kept[0]

    def make_output(after):
        v.output_own = output_rows(v.middle, v.down_own, v.down_peer, b_down_row, after)
        v.output_other = swap(v.output_own)
        return v.output_own

    def gradient_of_rows(after):
        v.grad_inputs_own, v.sums_one = input_gradient(
            own, v.gn_one_own, v.gn_one_peer, inputs, v.middles_own, gain_one, after)
        v.sums = call(bundle_kernel, "bundle", (1,), [(a, whole(a)) for a in (*v.sums_two, v.sums_one)],
                      [piece_spec((8, width))], 8, 0)[0]
        v.sums_peer = swap(v.sums)
        v.grad_inputs_other = swap(gate(v.grad_inputs_own, (v.sums,)))
        return v.sums

    def small_start(after):
        v.small = call(
            local_rows_kernel, "local_rows", (1,),
            [(a, whole(a)) for a in (v.sums, v.sums_peer, v.b_up_own, v.b_up_other, v.b_qv_own, v.b_qv_other)],
            [piece_spec((16, width))], 8, 0, after=after)[0]
        v.strides = [1 << i for i in range(dp_count.bit_length() - 1)]
        v.small_peer = exchange(v.small, v.strides.pop(0), dp_count)
        return v.small

    def small_step(after):
        v.small = add(1, v.small, v.small_peer, after=after)
        if v.strides:
            v.small_peer = exchange(v.small, v.strides.pop(0), dp_count)
        return v.small

    def place_down(after):
        [v.grad_w_down] = place_rows(bits, v.down.held, after)
        return v.grad_w_down

    def place_up(after):
        [v.grad_w_up] = place_rows(bits, v.up.held, after)
        return v.grad_w_up

    def place_heads(after):
        v.grad_w_heads, v.grad_w_out = place_attention(bits, v.heads.held, after)
        return v.grad_w_out

    def place_output(after):
        v.output = whole_rows(own, v.output_own, v.output_other, after)
        return v.output

    def place_inputs(after):
        v.grad_inputs = whole_rows(own, v.grad_inputs_own, v.grad_inputs_other, after)
        return v.grad_inputs

    step = lambda unit, name: lambda after: getattr(getattr(v, unit), name)(after)
    events = {
        "FFo": feed_other, "FFw": feed_own, "dWd": down_product, "dWu": up_product,
        "mda": lambda after: middle_half(0, after), "mdb": lambda after: middle_half(1, after),
        "bwo": backward_own, "dn": send_down, "bwt": backward_other, "dWa": heads_product, "or": make_output,
        "ig": gradient_of_rows, "s0": small_start, "s1": small_step, "s2": small_step, "s3": small_step, "s4": small_step,
        "Dp": place_down, "Up": place_up, "Ap": place_heads, "op": place_output, "ip": place_inputs,
    }
    for letter, unit in (("D", "down"), ("U", "up"), ("A", "heads")):
        for short, name in (("oc", "over_core"), ("oy", "over_y"), ("oz", "over_z"), ("t", "total"), ("by", "back_y"), ("bc", "back_core")):
            events[letter + short] = step(unit, name)
    last = None
    for name in ORDER:
        made = events[name.strip("*")](() if last is None or name.endswith("*") else (last,))
        last = last if made is None else made
    while v.strides:
        small_step(())
    output, grad_inputs, grad_w_heads, grad_w_out = v.output, v.grad_inputs, v.grad_w_heads, v.grad_w_out
    grad_w_up, grad_w_down, small = v.grad_w_up, v.grad_w_down, v.small
    return (
        output,
        grad_inputs,
        small[4],
        small[5],
        grad_w_heads.reshape(3, width, heads_width).transpose(1, 0, 2),
        small[15, : 2 * heads_width].reshape(2, heads_width),
        grad_w_out,
        small[2],
        small[0],
        small[1],
        grad_w_up,
        small[8 : 8 + units // width].reshape(units),
        grad_w_down,
        small[3],
    )


def solution(mesh):
    rows, copied, columns = P("dp", None), P(), P(None, "tensor")
    heads, split_rows = P(None, None, "tensor"), P("tensor", None)
    return jax.shard_map(
        functools.partial(shards, mesh.shape["dp"]),
        mesh=mesh,
        in_specs=(rows, rows, copied, copied, heads, columns, split_rows, copied, copied, copied, columns,
                  P("tensor"), split_rows, copied, rows),
        out_specs=(rows, rows, copied, copied, heads, columns, split_rows, copied, copied, copied, columns,
                   P("tensor"), split_rows, copied),
        check_vma=False,
    )
```

```python
import functools
import math
import types

import jax
import jax.numpy as jnp
from jax import lax
from jax.experimental import pallas as pl
from jax.experimental.pallas import tpu as pltpu
from jax.sharding import PartitionSpec as P

HEAD_DIM = 64
LANES = 128
EPS = 1e-06
MASKED = -1e30
MIB = 1024 * 1024
F32 = jnp.float32
BF16 = jnp.bfloat16
ERFC_P = 0.3925
ERFC_C = (
    0.2342248384381894,
    0.1104885068031651,
    0.6008554065531575,
    -0.5658356357906557,
    0.8411781949001069,
    -0.22091131771921121,
)


def dot(left, right):
    return lax.dot_general(left, right, (((1,), (0,)), ((), ())), preferred_element_type=F32)


def dot_bt(left, right):
    return lax.dot_general(left, right, (((1,), (1,)), ((), ())), preferred_element_type=F32)


def dot_at(left, right):
    return lax.dot_general(left, right, (((0,), (0,)), ((), ())), preferred_element_type=F32)


def standardize(values):
    row_mean = jnp.mean(values, -1, keepdims=True)
    centred = values - row_mean
    inverse_deviation = lax.rsqrt(jnp.mean(centred * centred, -1, keepdims=True) + EPS)
    return centred * inverse_deviation, inverse_deviation


def norm_pull(grad_normed, gain, xhat, inverse_deviation):
    scaled = grad_normed * gain
    return inverse_deviation * (
        scaled
        - jnp.mean(scaled, -1, keepdims=True)
        - xhat * jnp.mean(scaled * xhat, -1, keepdims=True)
    )


def segment_bias(lengths_ref, seq, seq_len):
    end_one = lengths_ref[seq, 0]
    end_two = end_one + lengths_ref[seq, 1]
    end_three = end_two + lengths_ref[seq, 2]

    def ids(shape, dim):
        place = lax.broadcasted_iota(jnp.int32, shape, dim)
        return (
            (place >= end_one).astype(jnp.int32)
            + (place >= end_two).astype(jnp.int32)
            + (place >= end_three).astype(jnp.int32)
        )

    same = ids((seq_len, seq_len), 0) == ids((seq_len, seq_len), 1)
    return jnp.where(same, 0.0, MASKED).astype(F32)


def head_only(block, half):
    lane = lax.broadcasted_iota(jnp.int32, block.shape, 1)
    mine = (lane < HEAD_DIM) if half == 0 else (lane >= HEAD_DIM)
    return jnp.where(mine, block, jnp.zeros_like(block))


ANY = pl.BlockSpec(memory_space=pl.ANY)


def call(kernel, name, grid, inputs, outputs, vmem_mib, flops, prefetch=(), scratch=(), after=(), aliases=None):
    arrays, in_specs = [a for a, _ in inputs], [b for _, b in inputs]
    first = len(prefetch) + len(arrays)

    def body(*refs):
        kernel(*refs[:first], *refs[first + len(after) :])

    return pl.pallas_call(
        body,
        out_shape=tuple(jax.ShapeDtypeStruct(shape, dtype) for shape, dtype, _ in outputs),
        grid_spec=pltpu.PrefetchScalarGridSpec(
            num_scalar_prefetch=len(prefetch),
            grid=grid,
            in_specs=in_specs + [ANY] * len(after),
            out_specs=tuple(spec for _, _, spec in outputs),
            scratch_shapes=list(scratch),
        ),
        input_output_aliases=aliases or {},
        compiler_params=pltpu.CompilerParams(vmem_limit_bytes=vmem_mib * MIB),
        cost_estimate=pl.CostEstimate(flops=1, bytes_accessed=1, transcendentals=0),
        name=name,
    )(*prefetch, *arrays, *after)


def whole(array):
    shape = array if isinstance(array, tuple) else array.shape
    return pl.BlockSpec(shape, lambda *_: (0,) * len(shape))


def at_sequence(rows, columns):
    return pl.BlockSpec((rows, columns), lambda i, seq, *_: (seq[0], 0))


def attention_forward_kernel(
    seq_ref, lengths_ref, rows_ref, w_ref, b_ref, gain_ref, shift_ref,
    normed_ref, qkv_ref, attended_ref, lse_ref, bias_ref,
):
    seq_len = rows_ref.shape[0]
    width = w_ref.shape[2]
    xhat, _ = standardize(rows_ref[...])
    normed = (xhat * gain_ref[...] + shift_ref[...]).astype(BF16)
    normed_ref[...] = normed
    scale = 1.0 / math.sqrt(HEAD_DIM)
    qkv_ref[0] = ((dot(normed, w_ref[0]) + b_ref[0:1]).astype(BF16).astype(F32) * scale).astype(BF16)
    qkv_ref[1] = dot(normed, w_ref[1]).astype(BF16)
    qkv_ref[2] = (dot(normed, w_ref[2]) + b_ref[1:2]).astype(BF16)
    bias_ref[...] = segment_bias(lengths_ref, seq_ref[0], seq_len)
    lane = lax.broadcasted_iota(jnp.int32, (seq_len, LANES), 1)
    stats = jnp.zeros((seq_len, LANES), F32)
    for pair in range(width // LANES):
        cols = slice(pair * LANES, (pair + 1) * LANES)
        query, key, value = qkv_ref[0, :, cols], qkv_ref[1, :, cols], qkv_ref[2, :, cols]
        mixed = None
        for half in range(2):
            scores = dot_bt(query, head_only(key, half)) + bias_ref[...]
            row_max = jnp.max(scores, -1, keepdims=True)
            exps = jnp.exp(scores - row_max)
            total = jnp.sum(exps, -1, keepdims=True)
            probs = (exps * (1.0 / total)).astype(BF16)
            part = dot(probs, head_only(value, half))
            mixed = part if mixed is None else mixed + part
            stats = jnp.where(lane == 2 * pair + half, row_max + jnp.log(total), stats)
        attended_ref[:, cols] = mixed.astype(BF16).astype(F32)
    lse_ref[...] = stats.T[: lse_ref.shape[0]]


def feed_forward_kernel(
    seq_ref, rows_ref, cot_ref, att_mine_ref, att_peer_ref, wo_mine_ref, wo_peer_ref, b_out_ref,
    gain_ref, shift_ref, w_up_ref, b_up_ref, w_down_ref,
    middle_ref, normed_ref, hidden_ref, grad_pre_ref, down_ref, grad_normed_low, grad_normed_high, grad_b_up_ref,
):
    middle = (
        rows_ref[...]
        + dot(att_mine_ref[...].astype(BF16), wo_mine_ref[...])
        + dot(att_peer_ref[...].astype(BF16), wo_peer_ref[...].astype(BF16))
        + b_out_ref[...]
    )
    middle_ref[...] = middle
    xhat, _ = standardize(middle)
    normed = (xhat * gain_ref[...] + shift_ref[...]).astype(BF16)
    normed_ref[...] = normed
    cot = cot_ref[...].astype(BF16)

    @pl.when(pl.program_id(0) == 0)
    def _():
        grad_b_up_ref[...] = jnp.zeros_like(grad_b_up_ref)

    pre = dot(normed, w_up_ref[...]) + b_up_ref[...]
    size = jnp.abs(pre) * math.sqrt(0.5)
    t = 1.0 / (1.0 + ERFC_P * size)
    gauss = jnp.exp(-0.5 * (pre * pre))
    poly = ERFC_C[-1]
    for c in ERFC_C[-2::-1]:
        poly = poly * t + c
    tail = 0.5 * (poly * t) * gauss
    cdf = jnp.where(pre >= 0, 1.0 - tail, tail)
    hidden = (pre * cdf).astype(BF16)
    slope = cdf + pre * gauss * (1.0 / math.sqrt(2.0 * math.pi))
    hidden_ref[...] = hidden
    down_ref[...] = dot(hidden, w_down_ref[...])
    grad_pre = (dot_bt(cot, w_down_ref[...]) * slope).astype(BF16)
    grad_pre_ref[...] = grad_pre
    grad_b_up_ref[...] += jnp.sum(grad_pre.astype(F32), 0, keepdims=True)
    grad_normed = dot_bt(grad_pre, w_up_ref[...])

    @pl.when(pl.program_id(0) == 0)
    def _():
        grad_normed_low[...] = grad_normed

    @pl.when(pl.program_id(0) == 1)
    def _():
        grad_normed_high[...] = grad_normed


def middle_gradient_kernel(
    seq_ref, mine_ref, peer_ref, middle_ref, cot_ref, gain_ref, grad_middle_ref, sums_ref,
):
    grad_normed = mine_ref[...] + peer_ref[...]
    cot = cot_ref[...]
    xhat, inverse_deviation = standardize(middle_ref[...])
    grad_middle = cot + norm_pull(grad_normed, gain_ref[...], xhat, inverse_deviation)
    grad_middle_ref[...] = grad_middle

    def total(values):
        return jnp.sum(values, 0, keepdims=True)

    sums_ref[...] = jnp.concatenate(
        [total(grad_normed * xhat), total(grad_normed), total(grad_middle), total(cot)]
        + [jnp.zeros((4, cot.shape[1]), F32)],
        axis=0,
    )


def input_gradient_kernel(
    seq_ref, mine_ref, peer_ref, rows_ref, middle_low, middle_high, gain_ref, grad_rows_ref, sums_ref,
):
    grad_normed = mine_ref[...] + peer_ref[...]
    xhat, inverse_deviation = standardize(rows_ref[...])
    pulled = norm_pull(grad_normed, gain_ref[...], xhat, inverse_deviation)
    half = middle_low.shape[0]
    grad_rows_ref[0:half] = middle_low[...] + pulled[0:half]
    grad_rows_ref[half:] = middle_high[...] + pulled[half:]

    def total(values):
        return jnp.sum(values, 0, keepdims=True)

    sums_ref[...] = jnp.concatenate(
        [total(grad_normed * xhat), total(grad_normed), jnp.zeros((6, xhat.shape[1]), F32)], axis=0
    )


def attention_backward_kernel(
    seq_ref, lengths_ref, middle_low, middle_high, qkv_ref, lse_ref, w_out_ref, w_ref,
    grad_qkv_ref, grad_normed_ref, sums_ref, bias_ref, grad_att_ref,
):
    seq_len, width = grad_att_ref.shape
    half = middle_low.shape[0]
    grad_att_ref[0:half] = dot_bt(middle_low[...].astype(BF16), w_out_ref[...]).astype(BF16)
    grad_att_ref[half:] = dot_bt(middle_high[...].astype(BF16), w_out_ref[...]).astype(BF16)
    bias_ref[...] = segment_bias(lengths_ref, seq_ref[0], seq_len)
    scale = 1.0 / math.sqrt(HEAD_DIM)
    for pair in range(width // LANES):
        cols = slice(pair * LANES, (pair + 1) * LANES)
        query, key, value = qkv_ref[0, :, cols], qkv_ref[1, :, cols], qkv_ref[2, :, cols]
        grad_att = grad_att_ref[:, cols]
        grad_query = grad_key = grad_value = 0.0
        for half in range(2):
            head = 2 * pair + half
            key_half = head_only(key, half)
            scores = dot_bt(key_half, query) + bias_ref[...]
            probs = jnp.exp(scores - lse_ref[head : head + 1, :])
            grad_probs = dot_bt(head_only(value, half), grad_att)
            inner = jnp.sum(grad_probs * probs, 0, keepdims=True)
            grad_scores = (probs * (grad_probs - inner)).astype(BF16)
            grad_value += dot(probs.astype(BF16), head_only(grad_att, half))
            grad_key += dot(grad_scores, head_only(query, half))
            grad_query += dot_at(grad_scores, key_half)
        grad_qkv_ref[0, :, cols] = (grad_query * scale).astype(BF16)
        grad_qkv_ref[1, :, cols] = grad_key.astype(BF16)
        grad_qkv_ref[2, :, cols] = grad_value.astype(BF16)
    grad_normed_ref[...] = (
        dot_bt(grad_qkv_ref[0], w_ref[0]) + dot_bt(grad_qkv_ref[1], w_ref[1]) + dot_bt(grad_qkv_ref[2], w_ref[2])
    )
    sums_ref[...] = jnp.concatenate(
        [jnp.sum(grad_qkv_ref[0].astype(F32), 0, keepdims=True), jnp.sum(grad_qkv_ref[2].astype(F32), 0, keepdims=True)]
        + [jnp.zeros((6, width), F32)],
        axis=0,
    )


def attention_forward(seq, lengths, rows, w_heads, b_qv, gain, shift, seq_len, after=()):
    width, heads_width = rows.shape[1], w_heads.shape[2]
    stat_rows = 8 * pl.cdiv(heads_width // HEAD_DIM, 8)
    shapes = [((seq_len, width), BF16), ((3, seq_len, heads_width), BF16), ((seq_len, heads_width), F32), ((stat_rows, seq_len), F32)]
    return call(
        attention_forward_kernel, "attention_forward", (1,),
        [(rows, at_sequence(seq_len, width))] + [(a, whole(a)) for a in (w_heads, b_qv, gain, shift)],
        [(shape, dtype, whole(shape)) for shape, dtype in shapes],
        56, 2 * seq_len * heads_width * (3 * width + 8 * seq_len),
        prefetch=(seq, lengths), scratch=[pltpu.VMEM((seq_len, seq_len), F32)], after=after,
    )


def feed_forward(seq, rows, cot, att_mine, att_peer, wo_mine, wo_peer, b_out, gain, shift, w_up, b_up, w_down, seq_len, after=()):
    width, units = w_up.shape
    heads_width = att_mine.shape[1]
    steps = 2
    step = seq_len // steps
    local = lambda n: pl.BlockSpec((step, n), lambda i, s: (i, 0))
    chosen = pl.BlockSpec((step, width), lambda i, s: (s[0] * steps + i, 0))
    made = lambda n, dtype: ((seq_len, n), dtype, local(n))
    return call(
        feed_forward_kernel, "feed_forward", (steps,),
        [(rows, chosen), (cot, chosen), (att_mine, local(heads_width)), (att_peer, local(heads_width))]
        + [(a, whole(a)) for a in (wo_mine, wo_peer, b_out, gain, shift, w_up, b_up, w_down)],
        [made(width, F32), made(width, BF16), made(units, BF16), made(units, BF16), made(width, F32),
         piece_spec((step, width)), piece_spec((step, width)), ((1, units), F32, whole((1, units)))],
        44, 2 * seq_len * width * (4 * units + 2 * heads_width),
        prefetch=(seq,), after=after,
    )


def middle_gradient(blocks, mine, peer, middle, cotangent, gain, after=()):
    rows, width = mine.shape
    picked = lambda n: pl.BlockSpec((rows, width), lambda i, b: (b[n], 0))
    return call(
        middle_gradient_kernel, "middle_gradient", (1,),
        [(mine, whole(mine)), (peer, whole(peer)), (middle, picked(0)), (cotangent, picked(1)), (gain, whole(gain))],
        [piece_spec((rows, width)), piece_spec((8, width))],
        28, 20 * rows * width, prefetch=(blocks,), after=after,
    )


def input_gradient(seq, mine, peer, inputs, middles, gain, after=()):
    rows, width = mine.shape
    return call(
        input_gradient_kernel, "input_gradient", (1,),
        [(mine, whole(mine)), (peer, whole(peer)), (inputs, at_sequence(rows, width))] + [(a, whole(a)) for a in (*middles, gain)],
        [piece_spec((rows, width)), piece_spec((8, width))],
        28, 20 * rows * width, prefetch=(seq,), after=after,
    )


def attention_backward(seq, lengths, middles, qkv, lse, w_out, w_heads, after=()):
    seq_len, width = qkv.shape[1], w_out.shape[1]
    heads_width = w_heads.shape[2]
    return call(
        attention_backward_kernel, "attention_backward", (1,),
        [(a, whole(a)) for a in (*middles, qkv, lse, w_out, w_heads)],
        [(shape, dtype, whole(shape)) for shape, dtype in
         (((3, seq_len, heads_width), BF16), ((seq_len, width), F32), ((8, heads_width), F32))],
        34, 2 * seq_len * heads_width * (4 * width + 20 * seq_len),
        prefetch=(seq, lengths), after=after,
        scratch=[pltpu.VMEM((seq_len, seq_len), F32), pltpu.VMEM((seq_len, heads_width), BF16)],
    )


def swap(values):
    return lax.ppermute(values, "tensor", [(0, 1), (1, 0)])


def exchange(values, stride, count):
    return lax.ppermute(values, "dp", [(i, i ^ stride) for i in range(count)])


def piece_spec(shape):
    return shape, F32, whole(shape)


def quarter_start(bits_ref, kept, dy, dz, quarter):
    core, y, z = bits_ref[0], bits_ref[1], bits_ref[2]
    core = core if kept else 1 - core
    return ((core * 2 + (1 - y if dy else y)) * 2 + (1 - z if dz else z)) * quarter


def quarters(kept):
    return [(kept, dy, dz) for dy, dz in ((1, 1), (1, 0), (0, 1), (0, 0))]


def put_pieces(bits_ref, half_ref, kept, pieces):
    quarter = half_ref.shape[0] // 4
    y, z = bits_ref[1], bits_ref[2]
    each = len(pieces) // 4
    for k, (_, dy, dz) in enumerate(quarters(kept)):
        start = ((1 - y if dy else y) * 2 + (1 - z if dz else z)) * quarter
        for sub in range(each):
            size = quarter // each
            pieces[k * each + sub][...] = half_ref[pl.ds(pl.multiple_of(start + sub * size, 8), size)]


def weight_gradient_kernel(bits_ref, side_ref, left_own, left_other, right_own, right_other, *refs):
    pieces, half_ref = refs[:-1], refs[-1]
    own, other = right_own[...].astype(BF16), right_other[...].astype(BF16)
    rows = half_ref.shape[0]
    for kept in range(2):
        core = bits_ref[0] if kept else 1 - bits_ref[0]
        cols = pl.ds(pl.multiple_of(core * rows, LANES), rows)
        half_ref[...] = dot_at(left_own[:, cols], own) + dot_at(left_other[:, cols], other)
        put_pieces(bits_ref, half_ref, kept, pieces[-4:] if kept else pieces[:-4])


SUB = 1


def piece_outputs(rows, columns):
    return [piece_spec((rows // 8 // SUB, columns))] * (4 * SUB) + [piece_spec((rows // 8, columns))] * 4


def weight_gradient(bits, side, lefts, rights, seq_len, name, after=()):
    pair = isinstance(rights, tuple)
    own, other = rights if pair else (rights, rights)
    rows, columns = lefts[0].shape[1], own.shape[1]
    left = whole(lefts[0])
    right_own = pl.BlockSpec((seq_len, columns), lambda i, b, s: (0 if pair else s[0], 0))
    right_other = pl.BlockSpec((seq_len, columns), lambda i, b, s: (0 if pair else 1 - s[0], 0))
    made = call(
        weight_gradient_kernel, name, (1,),
        [(lefts[0], left), (lefts[1], left), (own, right_own), (other, right_other)],
        piece_outputs(rows, columns), 40, 4 * seq_len * rows * columns, prefetch=(bits, side), after=after,
        scratch=[pltpu.VMEM((rows // 2, columns), F32)],
    )
    return made[:-4], made[-4:]


def attention_weight_gradients_kernel(
    bits_ref, normed_own, normed_other, qkv_own, qkv_other, att_own, att_other, own_low, own_high, other_low, other_high, *pieces,
):
    side = pieces[-1].shape[0]
    low, high = slice(0, own_low.shape[0]), slice(own_low.shape[0], None)
    out_terms = ((att_own, low, own_low), (att_own, high, own_high), (att_other, low, other_low), (att_other, high, other_high))
    for kept in range(2):
        for k, which in enumerate(quarters(kept)):
            targets = pieces[-4 + k :][:1] if kept else pieces[k * SUB : (k + 1) * SUB]
            block = quarter_start(bits_ref, *which, 1)
            cols = pl.ds(pl.multiple_of((block % 2) * side, LANES), side)

            def put(value):
                size = targets[0].shape[0]
                for sub, target in enumerate(targets):
                    target[...] = value[sub * size : (sub + 1) * size]

            @pl.when(block < 6)
            def _():
                j = jnp.minimum(block // 2, 2)
                put(dot_at(normed_own[:, cols], qkv_own[j]) + dot_at(normed_other[:, cols], qkv_other[j]))

            @pl.when(block >= 6)
            def _():
                put(sum(dot_at(att[rows].astype(BF16), middle[:, cols].astype(BF16)) for att, rows, middle in out_terms))


def attention_weight_gradients(bits, normeds, qkvs, atts, middles, after=()):
    seq_len, side = atts[0].shape
    made = call(
        attention_weight_gradients_kernel, "attention_weight_gradients", (1,),
        [(a, whole(a)) for a in (*normeds, *qkvs, *atts, *middles)],
        piece_outputs(8 * side, side), 40, 32 * seq_len * side * side, prefetch=(bits,), after=after,
    )
    return made[:-4], made[-4:]


def first_add_kernel(*refs):
    kept, got, sums = refs[:4], refs[4:-4], refs[-4:]
    each = len(got) // 4
    for k in range(4):
        size = got[0].shape[0]
        for sub in range(each):
            rows = pl.ds(sub * size, size)
            sums[k][rows] = kept[k][rows] + got[k * each + sub][...]


def first_add(kept, got, after=()):
    arrays = (*kept, *got)
    return call(first_add_kernel, "first_add", (1,), [(a, whole(a)) for a in arrays], [piece_spec(a.shape) for a in kept],
                24, 1, after=after)


def add_kernel(count, *refs):
    sums = refs[count:]
    for k, ref in enumerate(sums):
        total = refs[k][...]
        for more in refs[k + len(sums) : count : len(sums)]:
            total = total + more[...]
        ref[...] = total


def add(outs, *arrays, after=()):
    made = call(functools.partial(add_kernel, len(arrays)), "add", (1,), [(a, whole(a)) for a in arrays],
                [piece_spec(arrays[k].shape) for k in range(outs)], 24, 1, after=after)
    return made if outs > 1 else made[0]


def place_kernel(at, numbers, kept, prefetched_ref, *refs):
    count = len(numbers)
    outs, sems = refs[count + kept : -1], refs[-1]

    def copies():
        for k, number in enumerate(numbers):
            for wanted, target, place in at(prefetched_ref, number):
                yield wanted, pltpu.make_async_copy(refs[k], outs[target].at[place], sems.at[k])

    for wanted, copy in copies():
        if wanted is None:
            copy.start()
        else:
            pl.when(wanted)(copy.start)
    for wanted, copy in copies():
        if wanted is None:
            copy.wait()
        else:
            pl.when(wanted)(copy.wait)


def place_pieces(at, prefetched, pieces, shapes, into=(), after=()):
    arrays = list(pieces.values())
    return call(
        functools.partial(place_kernel, at, list(pieces), len(into)), "place_pieces", (1,),
        [(p, whole(p)) for p in arrays] + [(a, ANY) for a in into],
        [(shape, F32, ANY) for shape in shapes], 24, 0, prefetch=(prefetched,),
        scratch=[pltpu.SemaphoreType.DMA((len(arrays),))], after=after,
        aliases={1 + len(arrays) + k: k for k in range(len(into))},
    )


def piece_number(bits_ref, k):
    core, y, z = bits_ref[0], bits_ref[1], bits_ref[2]
    flip = lambda bit, on: 1 - bit if on else bit
    return (flip(core, k & 4) * 2 + flip(y, k & 2)) * 2 + flip(z, k & 1)


def place_rows(bits, pieces, after=()):
    rows, columns = pieces[0].shape

    def at(bits_ref, k):
        return [(None, 0, pl.ds(pl.multiple_of(piece_number(bits_ref, k) * rows, 8), rows))]

    return place_pieces(at, bits, dict(enumerate(pieces)), [(8 * rows, columns)], (), after)


def place_attention(bits, pieces, into=(), after=()):
    side = next(iter(pieces.values())).shape[0]

    def at(bits_ref, k):
        number = piece_number(bits_ref, k)
        return [
            (number < 6, 0, jnp.minimum(number, 5)),
            (number == 6, 1, (pl.ds(0, side), pl.ds(0, side))),
            (number == 7, 1, (pl.ds(0, side), pl.ds(side, side))),
        ]

    return place_pieces(at, bits, pieces, [(6, side, side), (side, 2 * side)], into, after)


def whole_rows(own, pieces, into=(), after=()):
    rows, columns = next(iter(pieces.values())).shape

    def at(own_ref, k):
        which = own_ref[0] if k == 0 else 1 - own_ref[0]
        return [(None, 0, pl.ds(pl.multiple_of(which * rows, 8), rows))]

    return place_pieces(at, own, pieces, [(2 * rows, columns)], into, after)


def output_kernel(middle_ref, mine_ref, peer_ref, b_ref, output_ref):
    output_ref[...] = middle_ref[...] + (mine_ref[...] + peer_ref[...]) + b_ref[...]


def output_rows(middle, mine, peer, b_down, after=()):
    rows, width = middle.shape
    block = pl.BlockSpec((rows // 4, width), lambda i: (i, 0))
    return call(output_kernel, "output_rows", (4,), [(middle, block), (mine, block), (peer, block), (b_down, whole(b_down))],
                [(middle.shape, F32, block)], 16, 3 * middle.size, after=after)[0]


def gate(value, after):
    return call(lambda *refs: None, "gate", (1,), [(value, ANY)], [(value.shape, value.dtype, ANY)], 8, 0, after=after,
                aliases={0: 0})[0]


class DpSum:
    def __init__(self, count, halves):
        self.count = count
        self.kept = halves[1]
        self.flying = [exchange(piece, 1, count) for piece in halves[0]]

    def over_core(self, after=()):
        self.ya, self.yb, self.ka, self.kb = first_add(self.kept, self.flying, after)
        self.ya = exchange(self.ya, 2, self.count)
        self.yb = exchange(self.yb, 2, self.count)
        return self.kb

    def over_y(self, after=()):
        sent = add(1, self.ka, self.ya, after=after)
        self.flying = exchange(sent, 4, self.count)
        return sent

    def over_z(self, after=()):
        self.mine = add(1, self.kb, self.yb, self.flying, after=after)
        self.strides = [1 << i for i in range(3, self.count.bit_length() - 1)]
        self.flying = exchange(self.mine, self.strides.pop(0), self.count)
        return self.mine

    def total(self, after=()):
        self.mine = add(1, self.mine, self.flying, after=after)
        while self.strides:
            self.mine = add(1, self.mine, exchange(self.mine, self.strides.pop(0), self.count))
        self.held = [self.mine, exchange(self.mine, 4, self.count)]
        self.held += [exchange(self.mine, 2, self.count)]
        return self.mine

    def back_y(self, after=()):
        if after:
            self.held[1] = gate(self.held[1], after)
        self.held += [exchange(self.held[1], 2, self.count)]
        self.held += [exchange(self.held[k], 1, self.count) for k in range(2)]
        return self.held[1]

    def back_core(self, after=()):
        if after:
            self.held[2] = gate(self.held[2], after)
        self.held += [exchange(self.held[k], 1, self.count) for k in (2, 3)]
        return self.held[2]


def bundle_kernel(two_low, two_high, one_ref, sums_ref):
    two = two_low[0:4] + two_high[0:4]
    sums_ref[...] = jnp.concatenate([two, one_ref[0:2], jnp.zeros_like(one_ref[0:2])], axis=0)


def local_rows_kernel(mine_ref, peer_ref, up_own, up_other, qv_own, qv_other, sums_ref):
    width, side = mine_ref.shape[1], qv_own.shape[1]
    sums_ref[...] = jnp.zeros_like(sums_ref)
    sums_ref[0:8] = mine_ref[...] + peer_ref[...]
    up = up_own[...] + up_other[...]
    for j in range(up.shape[1] // width):
        sums_ref[8 + j : 9 + j] = up[:, j * width : (j + 1) * width]
    qv = qv_own[...] + qv_other[...]
    sums_ref[15:16, 0:side] = qv[0:1]
    sums_ref[15:16, side : 2 * side] = qv[1:2]


ORDER = (
    "FFo", "FFw*", "mda", "dWd", "dWu", "Doc", "mdb", "Doy*", "bwo*", "Uoc", "bwt", "Doz", "dWa*", "Aoc", "Uoy*",
    "dn*", "or*", "Dt", "Uoz*", "Aoy", "Dby", "Ut", "Aoz", "Uby", "Ubc*", "ig", "Dbc", "s0", "At", "Aby", "s1",
    "Aq", "op*", "iq", "Abc", "Dp", "s2*", "Up", "s3*", "ip*", "Ap*", "s4",
)


def shards(dp_count, inputs, pair_lengths, first_norm_gain, first_norm_bias, w_qkv, b_qv, w_out, b_out,
           second_norm_gain, second_norm_bias, w_up, b_up, w_down, b_down, cotangent):
    seq_count = pair_lengths.shape[0]
    token_count, width = inputs.shape
    seq_len = token_count // seq_count
    heads_width = w_qkv.shape[2]
    units = w_up.shape[1]
    side = lax.axis_index("tensor")
    place = lax.axis_index("dp")
    own, other = side.astype(jnp.int32).reshape(1), (1 - side).astype(jnp.int32).reshape(1)
    core = place % 2
    bits = jnp.stack([core, (place // 2) % 2, (place // 4) % 2]).astype(jnp.int32)
    w_heads = w_qkv.transpose(1, 0, 2)
    row = lambda v: v
    gain_one, shift_one, gain_two, shift_two = map(row, (first_norm_gain, first_norm_bias, second_norm_gain, second_norm_bias))
    b_out_row, b_up_row, b_down_row = row(b_out), row(b_up), row(b_down)

    piece_rows = heads_width // 2
    piece = lax.dynamic_slice_in_dim(w_out, core * piece_rows, piece_rows, 0).astype(F32)
    piece = swap(piece)

    def forward(seq, after=()):
        return attention_forward(seq, pair_lengths, inputs, w_heads, b_qv, gain_one, shift_one, seq_len, after)

    normed_own, qkv_own, att_own, lse_own = forward(own)
    att_peer_other = swap(att_own)
    normed_other, qkv_other, att_other, lse_other = forward(other, (att_own,))
    piece = gate(piece, (att_other,))
    piece_two = exchange(piece, 1, dp_count)
    wo_peer = jnp.where(core == 0, jnp.concatenate([piece, piece_two]), jnp.concatenate([piece_two, piece]))
    att_peer_own = swap(att_other)
    v = types.SimpleNamespace()

    def feed(seq, att_mine, att_peer, after=()):
        return feed_forward(seq, inputs, cotangent, att_mine, att_peer, w_out, wo_peer, b_out_row, gain_two, shift_two,
                            w_up, b_up_row, w_down, seq_len, after)

    def feed_other(after):
        _, v.normed_two_other, v.hidden_other, v.grad_pre_other, v.down_other, low, high, v.b_up_other = feed(
            other, att_other, att_peer_other)
        v.gn_two_peer = swap(low), swap(high)
        return v.hidden_other

    def feed_own(after):
        v.middle, v.normed_two_own, v.hidden_own, v.grad_pre_own, v.down_own, low, high, v.b_up_own = feed(
            own, att_own, att_peer_own, after)
        v.gn_two_own = low, high
        return v.hidden_own

    def down_product(after):
        v.down = DpSum(dp_count, weight_gradient(
            bits, own, (v.hidden_own, v.hidden_other), cotangent, seq_len, "down_weight_gradient", after))
        return v.down.kept[0]

    def up_product(after):
        v.up = DpSum(dp_count, weight_gradient(
            bits, own, (v.normed_two_own, v.normed_two_other), (v.grad_pre_own, v.grad_pre_other), seq_len,
            "up_weight_gradient", after))
        return v.up.kept[0]

    v.middles_own, v.middles_other, v.sums_two = [], [], []

    def middle_half(half, after):
        blocks = jnp.concatenate([own * 0 + half, own * 2 + half])
        made, sums = middle_gradient(
            blocks, v.gn_two_own[half], v.gn_two_peer[half], v.middle, cotangent, gain_two, after)
        v.middles_own.append(made)
        v.middles_other.append(swap(made))
        v.sums_two.append(sums)
        return made

    def backward(seq, middles, qkv, lse, after):
        return attention_backward(seq, pair_lengths, middles, qkv, lse, w_out, w_heads, after)

    def backward_own(after):
        v.grad_qkv_own, v.gn_one_own, v.b_qv_own = backward(own, v.middles_own, qkv_own, lse_own, after)
        return v.gn_one_own

    def send_down(after):
        v.down_peer = swap(gate(v.down_other, after))

    def backward_other(after):
        v.grad_qkv_other, v.gn_one_other, v.b_qv_other = backward(other, v.middles_other, qkv_other, lse_other, after)
        v.gn_one_peer = swap(v.gn_one_other)
        return v.gn_one_other

    def heads_product(after):
        v.heads = DpSum(dp_count, attention_weight_gradients(
            bits, (normed_own, normed_other), (v.grad_qkv_own, v.grad_qkv_other), (att_own, att_other),
            (*v.middles_own, *v.middles_other), after))
        return v.heads.kept[0]

    def make_output(after):
        v.output_own = output_rows(v.middle, v.down_own, v.down_peer, b_down_row, after)
        v.output_other = swap(v.output_own)
        return v.output_own

    def gradient_of_rows(after):
        v.grad_inputs_own, v.sums_one = input_gradient(
            own, v.gn_one_own, v.gn_one_peer, inputs, v.middles_own, gain_one, after)
        v.sums = call(bundle_kernel, "bundle", (1,), [(a, whole(a)) for a in (*v.sums_two, v.sums_one)],
                      [piece_spec((8, width))], 8, 0)[0]
        v.sums_peer = swap(v.sums)
        v.grad_inputs_other = swap(gate(v.grad_inputs_own, (v.sums,)))
        return v.sums

    def small_start(after):
        v.small = call(
            local_rows_kernel, "local_rows", (1,),
            [(a, whole(a)) for a in (v.sums, v.sums_peer, v.b_up_own, v.b_up_other, v.b_qv_own, v.b_qv_other)],
            [piece_spec((16, width))], 8, 0, after=after)[0]
        v.strides = [1 << i for i in range(dp_count.bit_length() - 1)]
        v.small_peer = exchange(v.small, v.strides.pop(0), dp_count)
        return v.small

    def small_step(after):
        v.small = add(1, v.small, v.small_peer, after=after)
        if v.strides:
            v.small_peer = exchange(v.small, v.strides.pop(0), dp_count)
        return v.small

    def place_down(after):
        [v.grad_w_down] = place_rows(bits, v.down.held, after)
        return v.grad_w_down

    def place_up(after):
        [v.grad_w_up] = place_rows(bits, v.up.held, after)
        return v.grad_w_up

    def place_heads_early(after):
        v.heads_placed = place_attention(bits, {k: v.heads.held[k] for k in (0, 1, 2, 4, 5)}, (), after)
        return v.heads_placed[1]

    def place_heads(after):
        v.grad_w_heads, v.grad_w_out = place_attention(bits, {k: v.heads.held[k] for k in (3, 6, 7)}, v.heads_placed, after)
        return v.grad_w_out

    def place_output(after):
        [v.output] = whole_rows(own, {0: v.output_own, 1: v.output_other}, (), after)
        return v.output

    def place_inputs_early(after):
        v.inputs_placed = whole_rows(own, {0: v.grad_inputs_own}, (), after)
        return v.inputs_placed[0]

    def place_inputs(after):
        [v.grad_inputs] = whole_rows(own, {1: v.grad_inputs_other}, v.inputs_placed, after)
        return v.grad_inputs

    step = lambda unit, name: lambda after: getattr(getattr(v, unit), name)(after)
    events = {
        "FFo": feed_other, "FFw": feed_own, "dWd": down_product, "dWu": up_product,
        "mda": lambda after: middle_half(0, after), "mdb": lambda after: middle_half(1, after),
        "bwo": backward_own, "dn": send_down, "bwt": backward_other, "dWa": heads_product, "or": make_output,
        "ig": gradient_of_rows, "s0": small_start, "s1": small_step, "s2": small_step, "s3": small_step, "s4": small_step,
        "Dp": place_down, "Up": place_up, "Aq": place_heads_early, "Ap": place_heads, "op": place_output,
        "iq": place_inputs_early, "ip": place_inputs,
    }
    for letter, unit in (("D", "down"), ("U", "up"), ("A", "heads")):
        for short, name in (("oc", "over_core"), ("oy", "over_y"), ("oz", "over_z"), ("t", "total"), ("by", "back_y"), ("bc", "back_core")):
            events[letter + short] = step(unit, name)
    last = None
    for name in ORDER:
        made = events[name.strip("*")](() if last is None or name.endswith("*") else (last,))
        last = last if made is None else made
    while v.strides:
        small_step(())
    output, grad_inputs, grad_w_heads, grad_w_out = v.output, v.grad_inputs, v.grad_w_heads, v.grad_w_out
    grad_w_up, grad_w_down, small = v.grad_w_up, v.grad_w_down, v.small
    return (
        output,
        grad_inputs,
        small[4],
        small[5],
        grad_w_heads.reshape(3, width, heads_width).transpose(1, 0, 2),
        small[15, : 2 * heads_width].reshape(2, heads_width),
        grad_w_out,
        small[2],
        small[0],
        small[1],
        grad_w_up,
        small[8 : 8 + units // width].reshape(units),
        grad_w_down,
        small[3],
    )


def solution(mesh):
    rows, copied, columns = P("dp", None), P(), P(None, "tensor")
    heads, split_rows = P(None, None, "tensor"), P("tensor", None)
    return jax.shard_map(
        functools.partial(shards, mesh.shape["dp"]),
        mesh=mesh,
        in_specs=(rows, rows, copied, copied, heads, columns, split_rows, copied, copied, copied, columns,
                  P("tensor"), split_rows, copied, rows),
        out_specs=(rows, rows, copied, copied, heads, columns, split_rows, copied, copied, copied, columns,
                   P("tensor"), split_rows, copied),
        check_vma=False,
    )
```
